512 devices in a mesh: re: 16 (over y, core), pb: 32 (over x, z).
Axes of the slice: x: 4, y: 8, z: 8, core: 2. Of those that a mesh axis runs over, the one named last changes fastest.
Arguments:
- wannier_coupling: float32 [512, 4, 32, 3072], P('re', None, 'pb'), may hold values from -0.125 to 0.125
- electron_cells: int32 [3, 512], P(None, 're'), may hold values from -6 to 6
- phonon_cells: int32 [3, 4], replicated, may hold values from -6 to 6
- kpoint_coords: int32 [3, 8], replicated, may hold values from 0 to 7
- qpoint_coords: int32 [3, 128], replicated, may hold values from 0 to 7
- band_rotations: float32 [512, 2048], P('pb'), may hold values from -0.75 to 0.75
- mode_vectors: float32 [128, 4608], P('pb'), may hold values from -0.625 to 0.625
Outputs:
- coupling: float32 [8, 128, 32, 3072], P(None, 'pb', 're')
The draws below stay inside these ranges and needn't reach their ends.
All inputs are finite; a program needn't handle non-finite values.
Results may differ from the reference program's by a relative error of at most 0.000098.
Values sent between devices are 32-bit elements; how exact they have to be, the bound alone decides.
A program may use at most 64 MiB of HBM per device.

```python
import math
import jax
import jax.numpy as jnp
from jax import lax

NB = 32
NM = 48
RP = 4
K = 8
NF = 8
RE = 512
Q = 128
NG = 512


def place_ends(values, own_key, smallest, largest):
    place = [jax.random.randint(jax.random.fold_in(own_key, axis), (), 0, length) for axis, length in enumerate(values.shape)]
    widest = values.shape.index(max(values.shape))
    neighbour = place[:widest] + [(place[widest] + 1) % values.shape[widest]] + place[widest + 1:]
    return values.at[tuple(place)].set(smallest).at[tuple(neighbour)].set(largest)


def level_of(key, shape, shards, least, largest):
    gain, own = 1.0, jax.random.fold_in(key, 6)
    for position, parts in shards:
        draws = jnp.exp(jax.random.uniform(jax.random.fold_in(own, position), (parts,), jnp.float32, least / len(shards), largest / len(shards)))
        gain = gain * jnp.repeat(draws, shape[position] // parts).reshape([-1 if axis == position else 1 for axis in range(len(shape))])
    return gain


def bell_draw(stream_key, extent, width, limit, shards=(), held_as=jnp.bfloat16):
    array = width * jax.random.normal(stream_key, extent, jnp.float32)
    if shards:
        array = array * level_of(stream_key, extent, shards, -0.22, 0.18)
    return jnp.clip(array, -limit, limit).astype(held_as)


def setup_inputs(seed: int = 0) -> dict:
    streams_of = jax.random.split(jax.random.key(seed), 8)
    wannier_coupling = bell_draw(streams_of[0], (RE, RP, NB, 2 * NM * NB), (RE * RP) ** -0.5, 0.125, ((0, 16), (2, 32)), jnp.float32)
    electron_cells = place_ends(jax.random.randint(streams_of[1], (3, RE), -6, 7), jax.random.fold_in(streams_of[1], 1), -6, 6).astype(jnp.int32)
    phonon_cells = place_ends(jax.random.randint(streams_of[2], (3, RP), -6, 7), jax.random.fold_in(streams_of[2], 1), -6, 6).astype(jnp.int32)
    kpoint_coords = place_ends(jax.random.randint(streams_of[3], (3, K), 0, NF), jax.random.fold_in(streams_of[3], 1), 0, NF - 1).astype(jnp.int32)
    qpoint_coords = place_ends(jax.random.randint(streams_of[4], (3, Q), 0, NF), jax.random.fold_in(streams_of[4], 1), 0, NF - 1).astype(jnp.int32)
    band_rotations = bell_draw(streams_of[5], (NG, 2 * NB * NB), (2 * NB) ** -0.5, 0.75, ((0, 32),), jnp.float32)
    mode_vectors = bell_draw(streams_of[6], (Q, 2 * NM * NM), (2 * NM) ** -0.5, 0.625, ((0, 32),), jnp.float32)
    return dict(wannier_coupling=wannier_coupling, electron_cells=electron_cells, phonon_cells=phonon_cells, kpoint_coords=kpoint_coords, qpoint_coords=qpoint_coords, band_rotations=band_rotations, mode_vectors=mode_vectors)


highest = lax.Precision.HIGHEST


def grid_index(vectors):
    wrapped = jnp.mod(vectors, NF)
    return ((wrapped[0] * NF + wrapped[1]) * NF + wrapped[2]).astype(jnp.int32)


def complex_einsum(pattern, left_real, left_imag, right_real, right_imag):
    real_part = jnp.einsum(pattern, left_real, right_real, precision=highest) - jnp.einsum(pattern, left_imag, right_imag, precision=highest)
    imag_part = jnp.einsum(pattern, left_real, right_imag, precision=highest) + jnp.einsum(pattern, left_imag, right_real, precision=highest)
    return real_part, imag_part


def reference(wannier_coupling, electron_cells, phonon_cells, kpoint_coords, qpoint_coords, band_rotations, mode_vectors):
    phase_turns = jnp.mod(jnp.sum((2 * kpoint_coords[:, :, None] + 1) * electron_cells[:, None, :], axis=0), 2 * NF)
    phase_angle = phase_turns.astype(jnp.float32) * jnp.float32(math.pi / NF)
    blocks = wannier_coupling.reshape(RE, RP, NB, NM, 2, NB)
    cos_part = jnp.einsum("ke,epmacn->kpmacn", jnp.cos(phase_angle), blocks, precision=highest)
    sin_part = jnp.einsum("ke,epmacn->kpmacn", jnp.sin(phase_angle), blocks, precision=highest)
    bloch_real = cos_part[..., 0, :] - sin_part[..., 1, :]
    bloch_imag = cos_part[..., 1, :] + sin_part[..., 0, :]
    rotation_table = band_rotations.reshape(NG, 2, NB, NB)
    kpoint_rows = rotation_table[grid_index(kpoint_coords)]
    rot_real, rot_imag = complex_einsum("kpmaj,kjn->kpman", bloch_real, bloch_imag, kpoint_rows[:, 0], kpoint_rows[:, 1])
    qturns = jnp.mod(jnp.sum(qpoint_coords[:, :, None] * phonon_cells[:, None, :], axis=0), NF)
    qangle = qturns.astype(jnp.float32) * jnp.float32(2.0 * math.pi / NF)
    qcosine = jnp.cos(qangle)
    qsines = jnp.sin(qangle)
    pair_rows = grid_index(kpoint_coords[:, :, None] + qpoint_coords[:, None, :])
    mode_table = mode_vectors.reshape(Q, NM, 2, NM)

    def one_point(entries):
        part_real, part_imag, found_rows = entries
        phased_real, phased_imag = complex_einsum("qp,pman->qman", qcosine, qsines, part_real, part_imag)
        pair_vecs = rotation_table[found_rows]
        band_real, band_imag = complex_einsum("qmb,qman->qban", pair_vecs[:, 0], -pair_vecs[:, 1], phased_real, phased_imag)
        out_real, out_imag = complex_einsum("qban,qav->qnvb", band_real, band_imag, mode_table[:, :, 0], mode_table[:, :, 1])
        return jnp.stack([out_real, out_imag], axis=2).reshape(Q, NB, 2 * NM * NB)

    return lax.map(one_point, (rot_real, rot_imag, pair_rows))
```

```python
import math

import jax
import jax.numpy as jnp
from jax import lax
from jax.experimental import pallas as pl
from jax.experimental.pallas import tpu as pltpu
from jax.sharding import PartitionSpec as P

f32, bf16, i32 = jnp.float32, jnp.bfloat16, jnp.int32
MESH = pl.DeviceIdType.MESH
NN = ((1,), (0,))
NT = ((1,), (1,))


def split(value):
    high = value.astype(bf16)
    return high, (value - high.astype(f32)).astype(bf16)


def dot(left, right, dims):
    return lax.dot_general(left, right, (dims, ((), ())), preferred_element_type=f32)


def dot3(left, right, dims):
    return (
        dot(left[0], right[0], dims) + dot(left[1], right[0], dims) + dot(left[0], right[1], dims)
    )


def iota(shape, axis):
    return lax.broadcasted_iota(i32, shape, axis)


def wave(turns, period):
    cosine = jnp.zeros(turns.shape, f32)
    sine = jnp.zeros(turns.shape, f32)
    for step in range(period):
        hit = turns == step
        angle = 2 * math.pi * step / period
        cosine = jnp.where(hit, jnp.float32(math.cos(angle)), cosine)
        sine = jnp.where(hit, jnp.float32(math.sin(angle)), sine)
    return cosine, sine


def unfold(slices, wide):
    group = iota((16, 128), 1) >> 5
    for j in range(4):
        wide[pl.ds(j, 16, stride=4), :] = jnp.where(group == j, slices, 0.0)
    kept = wide[...]
    kept = kept + pltpu.roll(kept, 64, 1)
    return kept + pltpu.roll(kept, 32, 1)


def kernel(
    g_hbm, cells, pcell, kco, qco, rot_hbm, modes, out,
    g, acc, ra1, ra2, table, sel, usk, usq, wide, gkpad, a3s, a3r, xs,
    fq, fh, fl, bh, bl, xh, xl, ys,
    gsem, tsem, u1zs, u1zr, u1xs, u1xr, a1s_sem, a1r_sem, a2s_sem, a2r_sem,
    uks, ukr, uqs, uqr, ufs, ufr, a3s_sem, a3r_sem, bzs, bzr, bxs, bxr,
):
    re = lax.axis_index("re")
    pb = lax.axis_index("pb")
    y, core = re // 2, re % 2
    x, z = pb // 8, pb % 8

    def remote(src, dst, ssem, rsem, to_re, to_pb):
        return pltpu.make_async_remote_copy(
            src_ref=src, dst_ref=dst, send_sem=ssem, recv_sem=rsem,
            device_id=(to_re, to_pb), device_id_type=MESH,
        )

    def each(count, body):
        def step(i, carry):
            body(i)
            return carry

        lax.fori_loop(0, count, step, 0)

    g_copy = pltpu.make_async_copy(g_hbm, g, gsem.at[0])
    g_copy.start()
    own_rows = table.at[pl.ds(pl.multiple_of(pb * 16, 16), 16), :]
    t_copy = pltpu.make_async_copy(
        rot_hbm.at[:, pl.ds(pl.multiple_of(re * 128, 128), 128)], own_rows, tsem.at[0]
    )
    t_copy.start()

    barrier = pltpu.get_barrier_semaphore()

    def greet_re(d):
        pl.semaphore_signal(barrier, 1, device_id=((re + d + 1) % 16, pb), device_id_type=MESH)

    def greet_z(d):
        pl.semaphore_signal(
            barrier, 1, device_id=(re, x * 8 + (z + d + 1) % 8), device_id_type=MESH
        )

    def greet_x(d):
        pl.semaphore_signal(
            barrier, 1, device_id=(re, ((x + d + 1) % 4) * 8 + z), device_id_type=MESH
        )

    each(15, greet_re)
    each(7, greet_z)
    each(3, greet_x)

    row = iota((8, 32), 0)
    turns = jnp.zeros((8, 32), i32)
    for d in range(3):
        coef = jnp.zeros((8, 32), i32)
        for k in range(8):
            coef = jnp.where(row == k, 2 * kco[d, k] + 1, coef)
        turns = turns + coef * jnp.broadcast_to(cells[d : d + 1, :], (8, 32))
    cosine, sine = wave(turns & 15, 16)
    waves_h, waves_l = split(jnp.concatenate([cosine, sine], axis=0))
    waves = jnp.concatenate([waves_h, waves_l], axis=0)

    pl.semaphore_wait(barrier, 25)
    t_copy.wait()

    def u1z(d):
        return remote(
            own_rows, own_rows, u1zs.at[d], u1zr.at[z], re, x * 8 + (z + d + 1) % 8
        )

    each(7, lambda d: u1z(d).start())
    g_copy.wait()

    odd = ((iota((8, 128), 1) >> 5) & 1) == 1

    def phase_half(half):
        def step(i):
            for pp in range(2):
                highs, lows = [], []
                for lo in range(2):
                    start = half * 48 + pp * 24 + 2 * i + lo
                    high, low = split(g[pl.ds(start, 32, stride=96), :])
                    highs.append(high)
                    lows.append(low)
                high = jnp.concatenate(highs, axis=1)
                low = jnp.concatenate(lows, axis=1)
                first = dot(waves, high, NN)
                both = first[0:16] + first[16:32] + dot(waves_h, low, NN)
                for lo in range(2):
                    real = both[0:8, lo * 128 : lo * 128 + 128]
                    turned = both[8:16, lo * 128 : lo * 128 + 128]
                    swapped = jnp.where(
                        odd, pltpu.roll(turned, 32, 1), -pltpu.roll(turned, 96, 1)
                    )
                    acc[pl.ds(half * 384 + pp * 24 + lo * 12 + i, 8, stride=48), :] = (
                        real + swapped
                    )

        each(12, step)

    phase_half(1 - core)
    a1 = remote(
        acc.at[pl.ds(pl.multiple_of((1 - core) * 384, 8), 384), :], ra1,
        a1s_sem.at[0], a1r_sem.at[0], y * 2 + (1 - core), pb,
    )
    a1.start()
    phase_half(core)

    def z_rows(src):
        return table.at[pl.ds(pl.multiple_of((x * 8 + src) * 16, 16), 16), :]

    def wait_u1z(d):
        src = (z + d + 1) % 8
        remote(z_rows(src), z_rows(src), u1zs.at[0], u1zr.at[src], re, x * 8 + src).wait_recv()

    each(7, wait_u1z)

    def x_rows(src):
        return table.at[pl.ds(pl.multiple_of(src * 128, 128), 128), :]

    def u1x(d):
        return remote(x_rows(x), x_rows(x), u1xs.at[d], u1xr.at[x], re, ((x + d + 1) % 4) * 8 + z)

    each(3, lambda d: u1x(d).start())

    a1.wait_recv()
    mine = pl.multiple_of(core * 384, 8)
    ra1[...] = ra1[...] + acc[pl.ds(mine, 384), :]

    def block(ref, index):
        return ref.at[pl.ds(pl.multiple_of(index * 48, 8), 48), :]

    def a2(d):
        to = (y + d + 1) % 8
        return remote(block(ra1, to), block(ra2, y), a2s_sem.at[d], a2r_sem.at[y], to * 2 + core, pb)

    each(7, lambda d: a2(d).start())

    def wait_u1x(d):
        src = (x + d + 1) % 4
        remote(x_rows(src), x_rows(src), u1xs.at[0], u1xr.at[src], re, src * 8 + z).wait_recv()

    each(3, wait_u1x)

    for k in range(8):
        index = ((kco[0, k] & 7) * 8 + (kco[1, k] & 7)) * 8 + (kco[2, k] & 7)
        sel[k : k + 1, :] = table[pl.ds(index, 1), :]

    def choose(i):
        k, q = i // 4, pb * 4 + i % 4
        index = (
            ((kco[0, k] + qco[0, q]) & 7) * 8 + ((kco[1, k] + qco[1, q]) & 7)
        ) * 8 + ((kco[2, k] + qco[2, q]) & 7)
        sel[pl.ds(8 + i, 1), :] = table[pl.ds(index, 1), :]

    each(32, choose)

    def k_block(src):
        return usk.at[pl.ds(pl.multiple_of(src * 8, 8), 8), :]

    def q_block(src):
        return usq.at[pl.ds(pl.multiple_of(src * 32, 8), 32), :]

    def uk(d):
        return remote(sel.at[0:8, :], k_block(re), uks.at[d], ukr.at[re], (re + d + 1) % 16, pb)

    def uq(d):
        to = ((y + d + 1) % 8) * 2 + core
        return remote(sel.at[8:40, :], q_block(re), uqs.at[d], uqr.at[y], to, pb)

    each(15, lambda d: uk(d).start())
    each(7, lambda d: uq(d).start())
    usk[pl.ds(pl.multiple_of(re * 8, 8), 8), :] = sel[0:8, :]
    usq[pl.ds(pl.multiple_of(re * 32, 8), 32), :] = sel[8:40, :]

    def uf(i):
        src = i * 2 + core
        return remote(q_block(src), q_block(src), ufs.at[i], ufr.at[i], y * 2 + (1 - core), pb)

    lane12 = iota((12, 128), 1)
    permute_row = iota((96, 128), 0)
    block24 = (
        (permute_row >= 24).astype(i32)
        + (permute_row >= 48).astype(i32)
        + (permute_row >= 72).astype(i32)
    )
    rest = permute_row - 24 * block24
    part = (rest >= 12).astype(i32)
    target = part * 48 + 4 * (rest - 12 * part) + block24
    permute = (iota((96, 128), 1) == target).astype(f32).astype(bf16)

    def mode_q(q):
        v = [modes[pl.ds(tt * 4 + q, 12, stride=12), :] for tt in range(3)]
        r0, r1, r2 = pltpu.roll(v[0], 32, 1), pltpu.roll(v[1], 32, 1), pltpu.roll(v[1], 64, 1)
        r3, r4 = pltpu.roll(v[2], 64, 1), pltpu.roll(v[2], 96, 1)
        raw = [
            v[0],
            jnp.where(lane12 < 32, r0, r1),
            jnp.where(lane12 < 64, r2, r3),
            r4,
        ]
        plain, crossed = [], []
        for value in raw:
            value = jnp.where(lane12 < 96, value, 0.0)
            other = jnp.where(lane12 < 48, -pltpu.roll(value, 80, 1), pltpu.roll(value, 48, 1))
            plain.append(value)
            crossed.append(jnp.where(lane12 < 96, other, 0.0))
        point = pb * 4 + q
        for p in range(4):
            turn = (
                qco[0, point] * pcell[0, p]
                + qco[1, point] * pcell[1, p]
                + qco[2, point] * pcell[2, p]
            ) & 7
            cos_p, sin_p = wave(jnp.full((1, 128), turn, i32), 8)
            for a2 in range(2):
                for lo in range(2):
                    i = 2 * lo + a2
                    base = a2 * 192 + p * 24 + lo * 12
                    fq[base : base + 12, :] = cos_p * plain[i] + sin_p * crossed[i]
                    fq[base + 96 : base + 108, :] = cos_p * crossed[i] - sin_p * plain[i]
        high, low = split(fq[...])
        where = pl.ds(pl.multiple_of(q * 96, 96), 96)
        fh[where, :] = dot(permute, high, NT).astype(bf16)
        fl[where, :] = dot(permute, low, NT).astype(bf16)

    each(4, mode_q)

    def wait_uk(d):
        src = (re + d + 1) % 16
        remote(k_block(src), k_block(src), uks.at[0], ukr.at[src], src, pb).wait_recv()

    each(15, wait_uk)
    turned = unfold(usk[pl.ds(y, 16, stride=8), :], wide)
    real, imag = turned[0:32], turned[32:64]
    group = iota((32, 128), 1) >> 5
    pieces = []
    for a in range(2):
        pieces.append(jnp.where(group == 2 * a, real, jnp.where(group == 2 * a + 1, imag, 0.0)))
        pieces.append(jnp.where(group == 2 * a, -imag, jnp.where(group == 2 * a + 1, real, 0.0)))
    rotation = split(jnp.concatenate(pieces, axis=0))

    def wait_a2(d):
        src = (y + d + 1) % 8
        remote(block(ra2, src), block(ra2, src), a2s_sem.at[0], a2r_sem.at[src], re, pb).wait_recv()

    each(7, wait_a2)
    ra2[pl.ds(pl.multiple_of(y * 48, 8), 48), :] = ra1[pl.ds(pl.multiple_of(y * 48, 8), 48), :]
    total = ra2[0:48, :]
    for source in range(1, 8):
        total = total + ra2[source * 48 : source * 48 + 48, :]
    gkpad[...] = jnp.zeros_like(gkpad)
    gkpad[pl.ds(pl.multiple_of(core * 48, 8), 48), :] = total
    rotated = dot3(split(gkpad[...]), rotation, NN).T
    for ac in range(4):
        a3s[pl.ds(ac, 32, stride=4), :] = rotated[ac * 32 : ac * 32 + 32]

    def tile(ref, index):
        return ref.at[pl.ds(pl.multiple_of(index * 8, 8), 8), :]

    def a3(d):
        to = (re + d + 1) % 16
        return remote(tile(a3s, to), tile(a3r, re), a3s_sem.at[d], a3r_sem.at[re], to, pb)

    each(15, lambda d: a3(d).start())
    own_tile = pl.ds(pl.multiple_of(re * 8, 8), 8)
    a3r[own_tile, :] = a3s[own_tile, :]

    def wait_a3(d):
        src = (re + d + 1) % 16
        remote(tile(a3r, src), tile(a3r, src), a3s_sem.at[0], a3r_sem.at[src], src, pb).wait_recv()

    each(15, wait_a3)

    lane8 = iota((8, 128), 1)
    home = pl.multiple_of(pb * 48, 8)
    for n in range(2):
        v = [
            a3r[pl.ds(n * 4 + ac, 8, stride=16), :] + a3r[pl.ds(8 + n * 4 + ac, 8, stride=16), :]
            for ac in range(4)
        ]
        r1, r2, r3 = pltpu.roll(v[1], 96, 1), pltpu.roll(v[2], 64, 1), pltpu.roll(v[3], 32, 1)
        thirds = [
            jnp.where(lane8 < 96, v[0], r1),
            jnp.where(lane8 < 64, r1, r2),
            jnp.where(lane8 < 32, r2, r3),
        ]
        for t in range(3):
            for kh in range(2):
                xs[pl.ds(home + kh * 24 + t * 8 + n * 4, 4), :] = thirds[t][kh * 4 : kh * 4 + 4]

    def chunk(src, kh):
        return xs.at[pl.ds(pl.multiple_of(src * 48 + kh * 24, 8), 24), :]

    def bx(kh, zs, d):
        src = x * 8 + zs
        return remote(
            chunk(src, kh), chunk(src, kh), bxs.at[kh * 24 + zs * 3 + d], bxr.at[kh * 32 + src],
            re, ((x + d + 1) % 4) * 8 + z,
        )

    def bz(kh, d):
        return remote(
            chunk(pb, kh), chunk(pb, kh), bzs.at[kh * 7 + d], bzr.at[kh * 8 + z],
            re, x * 8 + (z + d + 1) % 8,
        )

    for kh in range(2):
        each(3, lambda d: bx(kh, z, d).start())
        each(7, lambda d: bz(kh, d).start())

    for kh in range(2):
        def pass_on(d):
            zs = (z + d + 1) % 8
            here = chunk(x * 8 + zs, kh)
            remote(here, here, bzs.at[0], bzr.at[kh * 8 + zs], re, pb).wait_recv()
            each(3, lambda e: bx(kh, zs, e).start())

        each(7, pass_on)

    uf_own = uf(y)
    uf_own.start()

    def wait_uq(d):
        src = (y + d + 1) % 8
        here = q_block(src * 2 + core)
        remote(here, here, uqs.at[0], uqr.at[src], re, pb).wait_recv()
        uf(src).start()

    each(7, wait_uq)

    def wait_uf(i):
        here = q_block(i * 2 + (1 - core))
        remote(here, here, ufs.at[0], ufr.at[i], re, pb).wait_recv()

    each(8, wait_uf)

    def pair_matrix(i):
        kk, q = i // 4, i % 4
        for kl in range(2):
            value = unfold(usq[pl.ds((2 * kk + kl) * 4 + q, 16, stride=32), :], wide)
            for part in range(2):
                for n in range(2):
                    kept = jnp.where(
                        group == 2 * kl + n, value[part * 32 : part * 32 + 32], 0.0
                    )
                    high, low = split(kept)
                    base = pl.multiple_of(i * 256 + part * 128 + kl * 64 + n * 32, 32)
                    bh[pl.ds(base, 32), :] = high
                    bl[pl.ds(base, 32), :] = low

    each(16, pair_matrix)

    group24 = iota((24, 128), 1) >> 5
    row96 = iota((96, 128), 0)
    first = (
        (row96 < 12)
        | ((row96 >= 24) & (row96 < 36))
        | ((row96 >= 48) & (row96 < 60))
        | ((row96 >= 72) & (row96 < 84))
    )
    for kh in range(2):
        def wait_bx(i):
            src = ((x + i // 8 + 1) % 4) * 8 + i % 8
            here = chunk(src, kh)
            remote(here, here, bxs.at[0], bxr.at[kh * 32 + src], re, pb).wait_recv()

        each(24, wait_bx)

        for k4 in range(4):
            for n in range(2):
                for t in range(3):
                    high, low = split(xs[pl.ds(kh * 24 + t * 8 + n * 4 + k4, 32, stride=48), :])
                    to = k4 * 64 + n * 32
                    xh[to : to + 32, t * 128 : t * 128 + 128] = high
                    xl[to : to + 32, t * 128 : t * 128 + 128] = low
        result = dot3((fh[...], fl[...]), (xh[...], xl[...]), NT)
        ys[0:384, :] = result[:, 0:128]
        ys[384:768, :] = result[:, 128:256]

        def finish(i):
            kk, q = i // 4, i % 4
            value = ys[pl.ds(pl.multiple_of(kk * 384 + q * 96, 8), 96), :]
            other = jnp.where(first, pltpu.roll(value, 84, 0), -pltpu.roll(value, 12, 0))
            left = split(jnp.concatenate([value, other], axis=1))
            where = pl.ds(pl.multiple_of(((kh * 2 + kk) * 4 + q) * 256, 256), 256)
            res = dot3(left, (bh[where, :], bl[where, :]), NN)
            quarter = [res[j * 24 : j * 24 + 24] for j in range(4)]
            for kl in range(2):
                for n in range(2):
                    to = 2 * kl + n
                    mixed = quarter[to]
                    for j in range(4):
                        if j != to:
                            shift = 32 * ((j - to) % 4)
                            mixed = jnp.where(
                                group24 == j, pltpu.roll(quarter[j], shift, 1), mixed
                            )
                    k = kh * 4 + kk * 2 + kl
                    out[pl.ds((k * 4 + q) * 48 + n, 24, stride=2), :] = mixed

        each(8, finish)

    each(7, lambda d: u1z(d).wait_send())
    each(3, lambda d: u1x(d).wait_send())
    a1.wait_send()
    each(7, lambda d: a2(d).wait_send())
    each(15, lambda d: uk(d).wait_send())
    each(7, lambda d: uq(d).wait_send())
    each(8, lambda d: uf(d).wait_send())
    each(15, lambda d: a3(d).wait_send())
    for kh in range(2):
        each(7, lambda d: bz(kh, d).wait_send())
        each(24, lambda i: bx(kh, i // 3, i % 3).wait_send())


def body(
    wannier_coupling,
    electron_cells,
    phonon_cells,
    kpoint_coords,
    qpoint_coords,
    band_rotations,
    mode_vectors,
):
    smem = pl.BlockSpec(memory_space=pltpu.SMEM)
    vmem = pl.BlockSpec(memory_space=pltpu.VMEM)
    hbm = pl.BlockSpec(memory_space=pl.ANY)
    V, D = pltpu.VMEM, pltpu.SemaphoreType.DMA
    result = pl.pallas_call(
        kernel,
        out_shape=jax.ShapeDtypeStruct((1536, 128), f32),
        in_specs=[hbm, vmem, smem, smem, smem, hbm, vmem],
        out_specs=vmem,
        scratch_shapes=[
            V((3072, 128), f32),
            V((768, 128), f32),
            V((384, 128), f32),
            V((384, 128), f32),
            V((512, 128), f32),
            V((40, 128), f32),
            V((128, 128), f32),
            V((512, 128), f32),
            V((64, 128), f32),
            V((128, 128), f32),
            V((128, 128), f32),
            V((128, 128), f32),
            V((1536, 128), f32),
            V((384, 128), f32),
            V((384, 384), bf16),
            V((384, 384), bf16),
            V((4096, 128), bf16),
            V((4096, 128), bf16),
            V((256, 384), bf16),
            V((256, 384), bf16),
            V((768, 128), f32),
            D((1,)), D((1,)), D((7,)), D((8,)), D((3,)), D((4,)), D((1,)), D((1,)),
            D((7,)), D((8,)), D((15,)), D((16,)), D((7,)), D((8,)), D((8,)), D((8,)),
            D((15,)), D((16,)), D((14,)), D((16,)), D((48,)), D((64,)),
        ],
        compiler_params=pltpu.CompilerParams(
            collective_id=0, has_side_effects=True, vmem_limit_bytes=40 * 1024 * 1024
        ),
        name="interpolate",
    )(
        wannier_coupling.reshape(3072, 128),
        electron_cells,
        phonon_cells,
        kpoint_coords,
        qpoint_coords,
        band_rotations,
        mode_vectors.reshape(4, 36, 128).transpose(1, 0, 2).reshape(144, 128),
    )
    return result.reshape(8, 4, 24, 2, 128).transpose(0, 1, 3, 2, 4).reshape(8, 4, 2, 3072)


def solution(mesh):
    return jax.shard_map(
        body,
        mesh=mesh,
        in_specs=(
            P("re", None, "pb", None),
            P(None, "re"),
            P(),
            P(),
            P(),
            P("pb", None),
            P("pb", None),
        ),
        out_specs=P(None, "pb", "re", None),
        check_vma=False,
    )
```

```python
import math

import jax
import jax.numpy as jnp
from jax import lax
from jax.experimental import pallas as pl
from jax.experimental.pallas import tpu as pltpu
from jax.sharding import PartitionSpec as P

f32, bf16, i32 = jnp.float32, jnp.bfloat16, jnp.int32
MESH = pl.DeviceIdType.MESH
NEAR = (0, 6, 1, 5, 2, 4, 3)
NEAR_X = (0, 2, 1)
NEAR_RE = (0, 14, 1, 13, 2, 12, 3, 11, 4, 10, 5, 9, 6, 8, 7)
NN = ((1,), (0,))
NT = ((1,), (1,))


def split(value):
    high = value.astype(bf16)
    return high, (value - high.astype(f32)).astype(bf16)


def dot(left, right, dims):
    return lax.dot_general(left, right, (dims, ((), ())), preferred_element_type=f32)


def dot3(left, right, dims):
    return (
        dot(left[0], right[0], dims) + dot(left[1], right[0], dims) + dot(left[0], right[1], dims)
    )


def iota(shape, axis):
    return lax.broadcasted_iota(i32, shape, axis)


def wave(turns, period):
    cosine = jnp.zeros(turns.shape, f32)
    sine = jnp.zeros(turns.shape, f32)
    for step in range(period):
        hit = turns == step
        angle = 2 * math.pi * step / period
        cosine = jnp.where(hit, jnp.float32(math.cos(angle)), cosine)
        sine = jnp.where(hit, jnp.float32(math.sin(angle)), sine)
    return cosine, sine


def unfold(slices, wide, region):
    group = iota((16, 128), 1) >> 5
    for j in range(4):
        wide[pl.ds(region * 64 + j, 16, stride=4), :] = jnp.where(group == j, slices, 0.0)
    kept = wide[region * 64 : region * 64 + 64, :]
    kept = kept + pltpu.roll(kept, 64, 1)
    return kept + pltpu.roll(kept, 32, 1)


def kernel(
    g_hbm, cells_hbm, pcell_hbm, kco_hbm, qco_hbm, rot_hbm, modes_hbm, out,
    cells, pcell, kco, qco, flat, modes, rot, g, acc, ra1, ra2, table, sel, kz, kx, usq, wide,
    gkpad, a3s, a3r, xs, fq, fh, fl, bh, bl, xh, xl, ys,
    gsem, rotsem, insem, u1zs, u1zr, u1xs, u1xr, a1s_sem, a1r_sem, a2s_sem, a2r_sem,
    kzs, kzr, kxs, kxr, uqs, uqr, ufs, ufr, a3s_sem, a3r_sem, bzs, bzr, bxs, bxr,
):
    re = lax.axis_index("re")
    pb = lax.axis_index("pb")
    y, core = re // 2, re % 2
    x, z = pb // 8, pb % 8

    def remote(src, dst, ssem, rsem, to_re, to_pb):
        return pltpu.make_async_remote_copy(
            src_ref=src, dst_ref=dst, send_sem=ssem, recv_sem=rsem,
            device_id=(to_re, to_pb), device_id_type=MESH,
        )

    def each(count, body):
        def step(i, carry):
            body(i)
            return carry

        lax.fori_loop(0, count, step, 0)

    small = [
        pltpu.make_async_copy(src, dst, insem.at[i])
        for i, (src, dst) in enumerate(
            [(kco_hbm, kco), (cells_hbm, cells), (pcell_hbm, pcell), (qco_hbm, qco)]
        )
    ]
    modes_copy = pltpu.make_async_copy(modes_hbm, flat, insem.at[4])

    def rot_copy(i):
        return pltpu.make_async_copy(
            rot_hbm.at[:, pl.ds(pl.multiple_of(i * 128, 128), 128)],
            rot.at[pl.ds(pl.multiple_of(i * 16, 16), 16), :],
            rotsem.at[i],
        )

    for copy in small:
        copy.start()
    g_copy = pltpu.make_async_copy(g_hbm, g, gsem.at[0])
    g_copy.start()
    each(16, lambda i: rot_copy(i).start())
    own_rows = table.at[pl.ds(pl.multiple_of(pb * 16, 16), 16), :]
    modes_copy.start()

    barrier = pltpu.get_barrier_semaphore()

    def greet_re(d):
        pl.semaphore_signal(barrier, 1, device_id=((re + d + 1) % 16, pb), device_id_type=MESH)

    def greet_z(d):
        pl.semaphore_signal(
            barrier, 1, device_id=(re, x * 8 + (z + d + 1) % 8), device_id_type=MESH
        )

    def greet_x(d):
        pl.semaphore_signal(
            barrier, 1, device_id=(re, ((x + d + 1) % 4) * 8 + z), device_id_type=MESH
        )

    for d in NEAR_RE[::-1]:
        greet_re(d)
    for d in NEAR[::-1]:
        greet_z(d)
    each(3, greet_x)
    for copy in small:
        copy.wait()

    row = iota((8, 64), 0)
    turns = jnp.zeros((8, 64), i32)
    twice = jnp.concatenate([cells[...], cells[...]], axis=1)
    for d in range(3):
        coef = jnp.zeros((8, 64), i32)
        for k in range(8):
            coef = jnp.where(row == k, 2 * kco[d, k] + 1, coef)
        turns = turns + coef * jnp.broadcast_to(twice[d : d + 1, :], (8, 64))
    cosine, sine = wave(turns & 15, 16)
    waves = jnp.concatenate(split(jnp.concatenate([cosine, sine], axis=0)), axis=0)

    k_index = ((kco[0, y] & 7) * 8 + (kco[1, y] & 7)) * 8 + (kco[2, y] & 7)
    each(16, lambda i: rot_copy(i).wait())
    held = jnp.full((16, 128), k_index >> 4, i32) == jnp.full((16, 128), pb, i32)

    def kz_block(src):
        return kz.at[pl.ds(pl.multiple_of(src * 16, 16), 16), :]

    def kx_block(src):
        return kx.at[pl.ds(pl.multiple_of(src * 16, 16), 16), :]

    kz[pl.ds(pl.multiple_of(z * 16, 16), 16), :] = jnp.where(
        held, rot[pl.ds(k_index & 15, 16, stride=16), :], 0.0
    )
    own_rows[...] = rot[pl.ds(pl.multiple_of(re * 16, 16), 16), :]

    odd = ((iota((8, 128), 1) >> 5) & 1) == 1

    def phase_part(half, pp):
        for i in range(12):
            highs, lows = [], []
            for lo in range(2):
                start = half * 48 + pp * 24 + 2 * i + lo
                high, low = split(g[pl.ds(start, 32, stride=96), :])
                highs.append(high)
                lows.append(low)
            stacked = jnp.concatenate(
                [jnp.concatenate(highs, axis=1), jnp.concatenate(lows, axis=1)], axis=0
            )
            both = dot(waves, stacked, NN)
            both = both[0:16] + both[16:32]
            for lo in range(2):
                real = both[0:8, lo * 128 : lo * 128 + 128]
                turned = both[8:16, lo * 128 : lo * 128 + 128]
                swapped = jnp.where(odd, pltpu.roll(turned, 32, 1), -pltpu.roll(turned, 96, 1))
                acc[pl.ds(half * 384 + pp * 24 + lo * 12 + i, 8, stride=48), :] = real + swapped

    g_copy.wait()
    for pp in range(2):
        phase_part(1 - core, pp)
    pl.semaphore_wait(barrier, 25)
    a1 = remote(
        acc.at[pl.ds(pl.multiple_of((1 - core) * 384, 8), 384), :], ra1,
        a1s_sem.at[0], a1r_sem.at[0], y * 2 + (1 - core), pb,
    )
    a1.start()

    def kz_copy(d):
        return remote(
            kz_block(z), kz_block(z), kzs.at[d], kzr.at[z], re, x * 8 + (z + d + 1) % 8
        )

    def u1z(d):
        return remote(
            own_rows, own_rows, u1zs.at[d], u1zr.at[z], re, x * 8 + (z + d + 1) % 8
        )

    for d in NEAR:
        kz_copy(d).start()
    for d in NEAR:
        u1z(d).start()
    for pp in range(2):
        phase_part(core, pp)

    a1.wait_recv()
    mine = pl.multiple_of(core * 384, 8)
    ra1[...] = ra1[...] + acc[pl.ds(mine, 384), :]

    def block(ref, index):
        return ref.at[pl.ds(pl.multiple_of(index * 48, 8), 48), :]

    def a2(d):
        to = (y + d + 1) % 8
        return remote(block(ra1, to), block(ra2, y), a2s_sem.at[d], a2r_sem.at[y], to * 2 + core, pb)

    for d in NEAR:
        a2(d).start()

    def wait_kz(d):
        src = (z + d + 1) % 8
        remote(kz_block(src), kz_block(src), kzs.at[0], kzr.at[src], re, pb).wait_recv()

    each(7, wait_kz)
    found = kz[0:16, :]
    for s in range(1, 8):
        found = found + kz[s * 16 : s * 16 + 16, :]
    kx[pl.ds(pl.multiple_of(x * 16, 16), 16), :] = found

    def kx_copy(d):
        return remote(
            kx_block(x), kx_block(x), kxs.at[d], kxr.at[x], re, ((x + d + 1) % 4) * 8 + z
        )

    each(3, lambda d: kx_copy(d).start())

    def z_rows(src):
        return table.at[pl.ds(pl.multiple_of((x * 8 + src) * 16, 16), 16), :]

    def wait_u1z(d):
        src = (z + d + 1) % 8
        remote(z_rows(src), z_rows(src), u1zs.at[0], u1zr.at[src], re, x * 8 + src).wait_recv()

    each(7, wait_u1z)

    def x_rows(src):
        return table.at[pl.ds(pl.multiple_of(src * 128, 128), 128), :]

    def u1x(d):
        return remote(x_rows(x), x_rows(x), u1xs.at[d], u1xr.at[x], re, ((x + d + 1) % 4) * 8 + z)

    each(3, lambda d: u1x(d).start())

    modes_copy.wait()
    for tile_index in range(36):
        modes[tile_index * 4 : tile_index * 4 + 4, :] = flat[
            :, tile_index * 128 : tile_index * 128 + 128
        ]
    lane12 = iota((12, 128), 1)
    permute_row = iota((96, 128), 0)
    block24 = (
        (permute_row >= 24).astype(i32)
        + (permute_row >= 48).astype(i32)
        + (permute_row >= 72).astype(i32)
    )
    rest = permute_row - 24 * block24
    part = (rest >= 12).astype(i32)
    target = part * 48 + 4 * (rest - 12 * part) + block24
    permute = (iota((96, 128), 1) == target).astype(f32).astype(bf16)

    def mode_q(q):
        v = [modes[pl.ds(tt * 4 + q, 12, stride=12), :] for tt in range(3)]
        r0, r1, r2 = pltpu.roll(v[0], 32, 1), pltpu.roll(v[1], 32, 1), pltpu.roll(v[1], 64, 1)
        r3, r4 = pltpu.roll(v[2], 64, 1), pltpu.roll(v[2], 96, 1)
        raw = [
            v[0],
            jnp.where(lane12 < 32, r0, r1),
            jnp.where(lane12 < 64, r2, r3),
            r4,
        ]
        plain, crossed = [], []
        for value in raw:
            value = jnp.where(lane12 < 96, value, 0.0)
            other = jnp.where(lane12 < 48, -pltpu.roll(value, 80, 1), pltpu.roll(value, 48, 1))
            plain.append(value)
            crossed.append(jnp.where(lane12 < 96, other, 0.0))
        point = pb * 4 + q
        for p in range(4):
            turn = (
                qco[0, point] * pcell[0, p]
                + qco[1, point] * pcell[1, p]
                + qco[2, point] * pcell[2, p]
            ) & 7
            cos_p, sin_p = wave(jnp.full((1, 128), turn, i32), 8)
            for a2 in range(2):
                for lo in range(2):
                    i = 2 * lo + a2
                    base = a2 * 192 + p * 24 + lo * 12
                    fq[base : base + 12, :] = cos_p * plain[i] + sin_p * crossed[i]
                    fq[base + 96 : base + 108, :] = cos_p * crossed[i] - sin_p * plain[i]
        high, low = split(fq[...])
        where = pl.ds(pl.multiple_of(q * 96, 96), 96)
        fh[where, :] = dot(permute, high, NT).astype(bf16)
        fl[where, :] = dot(permute, low, NT).astype(bf16)

    each(4, mode_q)

    def wait_kx(d):
        src = (x + d + 1) % 4
        remote(kx_block(src), kx_block(src), kxs.at[0], kxr.at[src], re, pb).wait_recv()

    each(3, wait_kx)
    k_row = kx[0:16, :] + kx[16:32, :] + kx[32:48, :] + kx[48:64, :]
    turned = unfold(k_row, wide, 0)
    real, imag = turned[0:32], turned[32:64]
    group = iota((32, 128), 1) >> 5
    pieces = []
    for a in range(2):
        pieces.append(jnp.where(group == 2 * a, real, jnp.where(group == 2 * a + 1, imag, 0.0)))
        pieces.append(jnp.where(group == 2 * a, -imag, jnp.where(group == 2 * a + 1, real, 0.0)))
    rotation = split(jnp.concatenate(pieces, axis=0))

    def wait_a2(d):
        src = (y + d + 1) % 8
        remote(block(ra2, src), block(ra2, src), a2s_sem.at[0], a2r_sem.at[src], re, pb).wait_recv()

    each(7, wait_a2)
    ra2[pl.ds(pl.multiple_of(y * 48, 8), 48), :] = ra1[pl.ds(pl.multiple_of(y * 48, 8), 48), :]
    total = ra2[0:48, :]
    for source in range(1, 8):
        total = total + ra2[source * 48 : source * 48 + 48, :]
    gkpad[...] = jnp.zeros_like(gkpad)
    gkpad[pl.ds(pl.multiple_of(core * 48, 8), 48), :] = total
    rotated = dot3(split(gkpad[...]), rotation, NN).T
    for ac in range(4):
        a3s[pl.ds(ac, 32, stride=4), :] = rotated[ac * 32 : ac * 32 + 32]

    def tile(ref, index):
        return ref.at[pl.ds(pl.multiple_of(index * 8, 8), 8), :]

    def a3(d):
        to = (re + d + 1) % 16
        return remote(tile(a3s, to), tile(a3r, re), a3s_sem.at[d], a3r_sem.at[re], to, pb)

    for d in NEAR_RE:
        a3(d).start()
    own_tile = pl.ds(pl.multiple_of(re * 8, 8), 8)
    a3r[own_tile, :] = a3s[own_tile, :]

    def wait_u1x(d):
        src = (x + d + 1) % 4
        remote(x_rows(src), x_rows(src), u1xs.at[0], u1xr.at[src], re, src * 8 + z).wait_recv()

    each(3, wait_u1x)

    def choose(i):
        k, q = i // 4, pb * 4 + i % 4
        index = (
            ((kco[0, k] + qco[0, q]) & 7) * 8 + ((kco[1, k] + qco[1, q]) & 7)
        ) * 8 + ((kco[2, k] + qco[2, q]) & 7)
        sel[pl.ds(i, 1), :] = table[pl.ds(index, 1), :]

    each(32, choose)

    def q_block(src):
        return usq.at[pl.ds(pl.multiple_of(src * 32, 8), 32), :]

    def uq(d):
        to = ((y + d + 1) % 8) * 2 + core
        return remote(sel, q_block(re), uqs.at[d], uqr.at[y], to, pb)

    for d in NEAR:
        uq(d).start()
    usq[pl.ds(pl.multiple_of(re * 32, 8), 32), :] = sel[...]

    def uf(i):
        src = i * 2 + core
        return remote(q_block(src), q_block(src), ufs.at[i], ufr.at[i], y * 2 + (1 - core), pb)

    def wait_a3(d):
        src = (re + d + 1) % 16
        remote(tile(a3r, src), tile(a3r, src), a3s_sem.at[0], a3r_sem.at[src], src, pb).wait_recv()

    each(15, wait_a3)

    lane8 = iota((8, 128), 1)
    home = pl.multiple_of(pb * 48, 8)
    for n in range(2):
        v = [
            a3r[pl.ds(n * 4 + ac, 8, stride=16), :] + a3r[pl.ds(8 + n * 4 + ac, 8, stride=16), :]
            for ac in range(4)
        ]
        r1, r2, r3 = pltpu.roll(v[1], 96, 1), pltpu.roll(v[2], 64, 1), pltpu.roll(v[3], 32, 1)
        thirds = [
            jnp.where(lane8 < 96, v[0], r1),
            jnp.where(lane8 < 64, r1, r2),
            jnp.where(lane8 < 32, r2, r3),
        ]
        for t in range(3):
            for kh in range(2):
                xs[pl.ds(home + kh * 24 + t * 8 + n * 4, 4), :] = thirds[t][kh * 4 : kh * 4 + 4]

    def chunk(src, kh):
        return xs.at[pl.ds(pl.multiple_of(src * 48 + kh * 24, 8), 24), :]

    def bx(kh, zs, d):
        src = x * 8 + zs
        return remote(
            chunk(src, kh), chunk(src, kh), bxs.at[kh * 24 + zs * 3 + d], bxr.at[kh * 32 + src],
            re, ((x + d + 1) % 4) * 8 + z,
        )

    def bz(kh, d):
        return remote(
            chunk(pb, kh), chunk(pb, kh), bzs.at[kh * 7 + d], bzr.at[kh * 8 + z],
            re, x * 8 + (z + d + 1) % 8,
        )

    for kh in range(2):
        for d in NEAR:
            bz(kh, d).start()
        for d in NEAR_X:
            bx(kh, z, d).start()

    for kh in range(2):
        def pass_on(d):
            zs = (z + d + 1) % 8
            here = chunk(x * 8 + zs, kh)
            remote(here, here, bzs.at[0], bzr.at[kh * 8 + zs], re, pb).wait_recv()
            for e in NEAR_X:
                bx(kh, zs, e).start()

        for d in NEAR:
            pass_on(d)

    uf_own = uf(y)
    uf_own.start()

    def wait_uq(d):
        src = (y + d + 1) % 8
        here = q_block(src * 2 + core)
        remote(here, here, uqs.at[0], uqr.at[src], re, pb).wait_recv()
        uf(src).start()

    for d in NEAR:
        wait_uq(d)

    def wait_uf(i):
        here = q_block(i * 2 + (1 - core))
        remote(here, here, ufs.at[0], ufr.at[i], re, pb).wait_recv()

    each(8, wait_uf)

    def pair_matrices(kk):
        for q in range(4):
            for kl in range(2):
                value = unfold(
                    usq[pl.ds((2 * kk + kl) * 4 + q, 16, stride=32), :], wide, q * 2 + kl
                )
                for part in range(2):
                    for n in range(2):
                        kept = jnp.where(
                            group == 2 * kl + n, value[part * 32 : part * 32 + 32], 0.0
                        )
                        high, low = split(kept)
                        base = pl.multiple_of(
                            (kk * 4 + q) * 256 + part * 128 + kl * 64 + n * 32, 32
                        )
                        bh[pl.ds(base, 32), :] = high
                        bl[pl.ds(base, 32), :] = low

    each(4, pair_matrices)

    group24 = iota((24, 128), 1) >> 5
    row96 = iota((96, 128), 0)
    first = (
        (row96 < 12)
        | ((row96 >= 24) & (row96 < 36))
        | ((row96 >= 48) & (row96 < 60))
        | ((row96 >= 72) & (row96 < 84))
    )
    for kh in range(2):
        def wait_bx(i):
            src = ((x + i // 8 + 1) % 4) * 8 + i % 8
            here = chunk(src, kh)
            remote(here, here, bxs.at[0], bxr.at[kh * 32 + src], re, pb).wait_recv()

        each(24, wait_bx)

        for k4 in range(4):
            for n in range(2):
                for t in range(3):
                    high, low = split(xs[pl.ds(kh * 24 + t * 8 + n * 4 + k4, 32, stride=48), :])
                    to = k4 * 64 + n * 32
                    xh[to : to + 32, t * 128 : t * 128 + 128] = high
                    xl[to : to + 32, t * 128 : t * 128 + 128] = low
        result = dot3((fh[...], fl[...]), (xh[...], xl[...]), NT)
        ys[0:384, :] = result[:, 0:128]
        ys[384:768, :] = result[:, 128:256]

        def finish(kk):
            for q in range(4):
                value = ys[pl.ds(pl.multiple_of(kk * 384 + q * 96, 8), 96), :]
                other = jnp.where(first, pltpu.roll(value, 84, 0), -pltpu.roll(value, 12, 0))
                left = split(jnp.concatenate([value, other], axis=1))
                where = pl.ds(pl.multiple_of(((kh * 2 + kk) * 4 + q) * 256, 256), 256)
                res = dot3(left, (bh[where, :], bl[where, :]), NN)
                quarter = [res[j * 24 : j * 24 + 24] for j in range(4)]
                for kl in range(2):
                    for n in range(2):
                        to = 2 * kl + n
                        mixed = quarter[to]
                        for j in range(4):
                            if j != to:
                                shift = 32 * ((j - to) % 4)
                                mixed = jnp.where(
                                    group24 == j, pltpu.roll(quarter[j], shift, 1), mixed
                                )
                        k = kh * 4 + kk * 2 + kl
                        out[pl.ds((k * 4 + q) * 48 + n, 24, stride=2), :] = mixed

        each(2, finish)

    each(7, lambda d: u1z(d).wait_send())
    each(3, lambda d: u1x(d).wait_send())
    a1.wait_send()
    each(7, lambda d: a2(d).wait_send())
    each(7, lambda d: kz_copy(d).wait_send())
    each(3, lambda d: kx_copy(d).wait_send())
    each(7, lambda d: uq(d).wait_send())
    each(8, lambda d: uf(d).wait_send())
    each(15, lambda d: a3(d).wait_send())
    for kh in range(2):
        each(7, lambda d: bz(kh, d).wait_send())
        each(24, lambda i: bx(kh, i // 3, i % 3).wait_send())


def body(
    wannier_coupling,
    electron_cells,
    phonon_cells,
    kpoint_coords,
    qpoint_coords,
    band_rotations,
    mode_vectors,
):
    hbm = pl.BlockSpec(memory_space=pltpu.HBM)
    vmem = pl.BlockSpec(memory_space=pltpu.VMEM)
    V, S, D = pltpu.VMEM, pltpu.SMEM, pltpu.SemaphoreType.DMA
    result = pl.pallas_call(
        kernel,
        out_shape=jax.ShapeDtypeStruct((1536, 128), f32),
        in_specs=[hbm] * 7,
        out_specs=vmem,
        scratch_shapes=[
            V((3, 32), i32),
            S((3, 4), i32),
            S((3, 8), i32),
            S((3, 128), i32),
            V((4, 4608), f32),
            V((144, 128), f32),
            V((256, 128), f32),
            V((3072, 128), f32),
            V((768, 128), f32),
            V((384, 128), f32),
            V((384, 128), f32),
            V((512, 128), f32),
            V((32, 128), f32),
            V((128, 128), f32),
            V((64, 128), f32),
            V((512, 128), f32),
            V((512, 128), f32),
            V((128, 128), f32),
            V((128, 128), f32),
            V((128, 128), f32),
            V((1536, 128), f32),
            V((384, 128), f32),
            V((384, 384), bf16),
            V((384, 384), bf16),
            V((4096, 128), bf16),
            V((4096, 128), bf16),
            V((256, 384), bf16),
            V((256, 384), bf16),
            V((768, 128), f32),
            D((1,)), D((16,)), D((5,)),
            D((7,)), D((8,)), D((3,)), D((4,)), D((1,)), D((1,)),
            D((7,)), D((8,)),
            D((7,)), D((8,)), D((3,)), D((4,)), D((7,)), D((8,)), D((8,)), D((8,)),
            D((15,)), D((16,)), D((14,)), D((16,)), D((48,)), D((64,)),
        ],
        compiler_params=pltpu.CompilerParams(
            collective_id=0, has_side_effects=True, vmem_limit_bytes=60 * 1024 * 1024
        ),
        name="interpolate",
    )(
        wannier_coupling.reshape(3072, 128),
        electron_cells,
        phonon_cells,
        kpoint_coords,
        qpoint_coords,
        band_rotations,
        mode_vectors,
    )
    return result.reshape(8, 4, 24, 2, 128).transpose(0, 1, 3, 2, 4).reshape(8, 4, 2, 3072)


def solution(mesh):
    return jax.shard_map(
        body,
        mesh=mesh,
        in_specs=(
            P("re", None, "pb", None),
            P(None, "re"),
            P(),
            P(),
            P(),
            P("pb", None),
            P("pb", None),
        ),
        out_specs=P(None, "pb", "re", None),
        check_vma=False,
    )
```

```python
import math

import jax
import jax.numpy as jnp
from jax import lax
from jax.experimental import pallas as pl
from jax.experimental.pallas import tpu as pltpu
from jax.sharding import PartitionSpec as P

f32, bf16, i32 = jnp.float32, jnp.bfloat16, jnp.int32
MESH = pl.DeviceIdType.MESH
NEAR = (0, 6, 1, 5, 2, 4, 3)
NEAR_X = (0, 2, 1)
NEAR_RE = (0, 14, 1, 13, 2, 12, 3, 11, 4, 10, 5, 9, 6, 8, 7)
NN = ((1,), (0,))
NT = ((1,), (1,))


def split(value):
    high = value.astype(bf16)
    return high, (value - high.astype(f32)).astype(bf16)


def dot(left, right, dims):
    return lax.dot_general(left, right, (dims, ((), ())), preferred_element_type=f32)


def dot3(left, right, dims):
    return (
        dot(left[0], right[0], dims) + dot(left[1], right[0], dims) + dot(left[0], right[1], dims)
    )


def iota(shape, axis):
    return lax.broadcasted_iota(i32, shape, axis)


def wave(turns, period):
    cosine = jnp.zeros(turns.shape, f32)
    sine = jnp.zeros(turns.shape, f32)
    for step in range(period):
        hit = turns == step
        angle = 2 * math.pi * step / period
        cosine = jnp.where(hit, jnp.float32(math.cos(angle)), cosine)
        sine = jnp.where(hit, jnp.float32(math.sin(angle)), sine)
    return cosine, sine


def unfold(slices, wide, region):
    group = iota((16, 128), 1) >> 5
    for j in range(4):
        wide[pl.ds(region * 64 + j, 16, stride=4), :] = jnp.where(group == j, slices, 0.0)
    kept = wide[region * 64 : region * 64 + 64, :]
    kept = kept + pltpu.roll(kept, 64, 1)
    return kept + pltpu.roll(kept, 32, 1)


def kernel(
    g_hbm, cells_hbm, pcell_hbm, kco_hbm, qco_hbm, rot_hbm, modes_hbm, out,
    cells, pcell, kco, qco, flat, modes, rot, g, acc, ra1, ra2, table, sel, kz, kx, usq, wide,
    a3s, a3r, xs, fq, fh, fl, bh, bl, xh, xl, ys,
    gsem, rotsem, insem, u1zs, u1zr, u1xs, u1xr, a1s_sem, a1r_sem, a2s_sem, a2r_sem,
    kzs, kzr, kxs, kxr, uqs, uqr, ufs, ufr, a3s_sem, a3r_sem, bzs, bzr, bxs, bxr,
):
    re = lax.axis_index("re")
    pb = lax.axis_index("pb")
    y, core = re // 2, re % 2
    x, z = pb // 8, pb % 8

    def remote(src, dst, ssem, rsem, to_re, to_pb):
        return pltpu.make_async_remote_copy(
            src_ref=src, dst_ref=dst, send_sem=ssem, recv_sem=rsem,
            device_id=(to_re, to_pb), device_id_type=MESH,
        )

    def each(count, body):
        def step(i, carry):
            body(i)
            return carry

        lax.fori_loop(0, count, step, 0)

    barrier = pltpu.get_barrier_semaphore()

    def greet_re(d):
        pl.semaphore_signal(barrier, 1, device_id=((re + d + 1) % 16, pb), device_id_type=MESH)

    def greet_z(d):
        pl.semaphore_signal(
            barrier, 1, device_id=(re, x * 8 + (z + d + 1) % 8), device_id_type=MESH
        )

    def greet_x(d):
        pl.semaphore_signal(
            barrier, 1, device_id=(re, ((x + d + 1) % 4) * 8 + z), device_id_type=MESH
        )

    for d in NEAR_RE[::-1]:
        greet_re(d)
    for d in NEAR[::-1]:
        greet_z(d)
    each(3, greet_x)
    small = [
        pltpu.make_async_copy(src, dst, insem.at[i])
        for i, (src, dst) in enumerate(
            [(kco_hbm, kco), (cells_hbm, cells), (pcell_hbm, pcell), (qco_hbm, qco)]
        )
    ]
    modes_copy = pltpu.make_async_copy(modes_hbm, flat, insem.at[4])

    def rot_copy(i):
        return pltpu.make_async_copy(
            rot_hbm.at[:, pl.ds(pl.multiple_of(i * 128, 128), 128)],
            rot.at[pl.ds(pl.multiple_of(i * 16, 16), 16), :],
            rotsem.at[i],
        )

    g_copy = pltpu.make_async_copy(g_hbm, g, gsem.at[0])
    g_copy.start()
    for copy in small:
        copy.start()
    each(16, lambda i: rot_copy(i).start())
    own_rows = table.at[pl.ds(pl.multiple_of(pb * 16, 16), 16), :]
    modes_copy.start()

    for copy in small:
        copy.wait()

    row = iota((8, 64), 0)
    turns = jnp.zeros((8, 64), i32)
    twice = jnp.concatenate([cells[...], cells[...]], axis=1)
    for d in range(3):
        coef = jnp.zeros((8, 64), i32)
        for k in range(8):
            coef = jnp.where(row == k, 2 * kco[d, k] + 1, coef)
        turns = turns + coef * jnp.broadcast_to(twice[d : d + 1, :], (8, 64))
    cosine, sine = wave(turns & 15, 16)
    waves = jnp.concatenate(split(jnp.concatenate([cosine, sine], axis=0)), axis=0)

    k_index = ((kco[0, y] & 7) * 8 + (kco[1, y] & 7)) * 8 + (kco[2, y] & 7)
    each(16, lambda i: rot_copy(i).wait())
    held = jnp.full((16, 128), k_index >> 4, i32) == jnp.full((16, 128), pb, i32)

    def kz_block(src):
        return kz.at[pl.ds(pl.multiple_of(src * 16, 16), 16), :]

    def kx_block(src):
        return kx.at[pl.ds(pl.multiple_of(src * 16, 16), 16), :]

    kz[pl.ds(pl.multiple_of(z * 16, 16), 16), :] = jnp.where(
        held, rot[pl.ds(k_index & 15, 16, stride=16), :], 0.0
    )
    own_rows[...] = rot[pl.ds(pl.multiple_of(re * 16, 16), 16), :]

    odd = ((iota((8, 128), 1) >> 5) & 1) == 1

    def phase_part(half, pp):
        for i in range(12):
            highs, lows = [], []
            for lo in range(2):
                start = half * 48 + pp * 24 + 2 * i + lo
                high, low = split(g[pl.ds(start, 32, stride=96), :])
                highs.append(high)
                lows.append(low)
            stacked = jnp.concatenate(
                [jnp.concatenate(highs, axis=1), jnp.concatenate(lows, axis=1)], axis=0
            )
            both = dot(waves, stacked, NN)
            both = both[0:16] + both[16:32]
            for lo in range(2):
                real = both[0:8, lo * 128 : lo * 128 + 128]
                turned = both[8:16, lo * 128 : lo * 128 + 128]
                swapped = jnp.where(odd, pltpu.roll(turned, 32, 1), -pltpu.roll(turned, 96, 1))
                acc[pl.ds(half * 384 + pp * 24 + lo * 12 + i, 8, stride=48), :] = real + swapped

    g_copy.wait()
    for pp in range(2):
        phase_part(1 - core, pp)
    for pp in range(2):
        phase_part(core, pp)
    pl.semaphore_wait(barrier, 25)
    a1 = remote(
        acc.at[pl.ds(pl.multiple_of((1 - core) * 384, 8), 384), :], ra1,
        a1s_sem.at[0], a1r_sem.at[0], y * 2 + (1 - core), pb,
    )
    a1.start()

    def kz_copy(d):
        return remote(
            kz_block(z), kz_block(z), kzs.at[d], kzr.at[z], re, x * 8 + (z + d + 1) % 8
        )

    def u1z(d):
        return remote(
            own_rows, own_rows, u1zs.at[d], u1zr.at[z], re, x * 8 + (z + d + 1) % 8
        )

    for d in NEAR:
        kz_copy(d).start()

    a1.wait_recv()
    mine = pl.multiple_of(core * 384, 8)
    ra1[...] = ra1[...] + acc[pl.ds(mine, 384), :]

    def block(ref, index):
        return ref.at[pl.ds(pl.multiple_of(index * 48, 8), 48), :]

    def a2(d):
        to = (y + d + 1) % 8
        return remote(block(ra1, to), block(ra2, y), a2s_sem.at[d], a2r_sem.at[y], to * 2 + core, pb)

    for d in NEAR:
        a2(d).start()
    for d in NEAR:
        u1z(d).start()

    def wait_kz(d):
        src = (z + d + 1) % 8
        remote(kz_block(src), kz_block(src), kzs.at[0], kzr.at[src], re, pb).wait_recv()

    each(7, wait_kz)
    found = kz[0:16, :]
    for s in range(1, 8):
        found = found + kz[s * 16 : s * 16 + 16, :]
    kx[pl.ds(pl.multiple_of(x * 16, 16), 16), :] = found

    def kx_copy(d):
        return remote(
            kx_block(x), kx_block(x), kxs.at[d], kxr.at[x], re, ((x + d + 1) % 4) * 8 + z
        )

    each(3, lambda d: kx_copy(d).start())

    def z_rows(src):
        return table.at[pl.ds(pl.multiple_of((x * 8 + src) * 16, 16), 16), :]

    def wait_u1z(d):
        src = (z + d + 1) % 8
        remote(z_rows(src), z_rows(src), u1zs.at[0], u1zr.at[src], re, x * 8 + src).wait_recv()

    each(7, wait_u1z)

    def x_rows(src):
        return table.at[pl.ds(pl.multiple_of(src * 128, 128), 128), :]

    def u1x(d):
        return remote(x_rows(x), x_rows(x), u1xs.at[d], u1xr.at[x], re, ((x + d + 1) % 4) * 8 + z)

    each(3, lambda d: u1x(d).start())

    modes_copy.wait()
    for tile_index in range(36):
        modes[tile_index * 4 : tile_index * 4 + 4, :] = flat[
            :, tile_index * 128 : tile_index * 128 + 128
        ]
    lane12 = iota((12, 128), 1)
    permute_row = iota((96, 128), 0)
    block24 = (
        (permute_row >= 24).astype(i32)
        + (permute_row >= 48).astype(i32)
        + (permute_row >= 72).astype(i32)
    )
    rest = permute_row - 24 * block24
    part = (rest >= 12).astype(i32)
    target = part * 48 + 4 * (rest - 12 * part) + block24
    permute = (iota((96, 128), 1) == target).astype(f32).astype(bf16)

    def mode_q(q):
        v = [modes[pl.ds(tt * 4 + q, 12, stride=12), :] for tt in range(3)]
        r0, r1, r2 = pltpu.roll(v[0], 32, 1), pltpu.roll(v[1], 32, 1), pltpu.roll(v[1], 64, 1)
        r3, r4 = pltpu.roll(v[2], 64, 1), pltpu.roll(v[2], 96, 1)
        raw = [
            v[0],
            jnp.where(lane12 < 32, r0, r1),
            jnp.where(lane12 < 64, r2, r3),
            r4,
        ]
        plain, crossed = [], []
        for value in raw:
            value = jnp.where(lane12 < 96, value, 0.0)
            other = jnp.where(lane12 < 48, -pltpu.roll(value, 80, 1), pltpu.roll(value, 48, 1))
            plain.append(value)
            crossed.append(jnp.where(lane12 < 96, other, 0.0))
        point = pb * 4 + q
        for p in range(4):
            turn = (
                qco[0, point] * pcell[0, p]
                + qco[1, point] * pcell[1, p]
                + qco[2, point] * pcell[2, p]
            ) & 7
            cos_p, sin_p = wave(jnp.full((1, 128), turn, i32), 8)
            for a2 in range(2):
                for lo in range(2):
                    i = 2 * lo + a2
                    base = a2 * 192 + p * 24 + lo * 12
                    fq[base : base + 12, :] = cos_p * plain[i] + sin_p * crossed[i]
                    fq[base + 96 : base + 108, :] = cos_p * crossed[i] - sin_p * plain[i]
        high, low = split(fq[...])
        where = pl.ds(pl.multiple_of(q * 96, 96), 96)
        fh[where, :] = dot(permute, high, NT).astype(bf16)
        fl[where, :] = dot(permute, low, NT).astype(bf16)

    each(4, mode_q)

    def wait_kx(d):
        src = (x + d + 1) % 4
        remote(kx_block(src), kx_block(src), kxs.at[0], kxr.at[src], re, pb).wait_recv()

    each(3, wait_kx)
    k_row = kx[0:16, :] + kx[16:32, :] + kx[32:48, :] + kx[48:64, :]
    turned = unfold(k_row, wide, 0)
    real, imag = turned[0:32], turned[32:64]
    group = iota((32, 128), 1) >> 5
    pieces = []
    for a in range(2):
        pieces.append(jnp.where(group == 2 * a, real, jnp.where(group == 2 * a + 1, imag, 0.0)))
        pieces.append(jnp.where(group == 2 * a, -imag, jnp.where(group == 2 * a + 1, real, 0.0)))
    rotation = split(jnp.concatenate(pieces, axis=0))

    def wait_a2(d):
        src = (y + d + 1) % 8
        remote(block(ra2, src), block(ra2, src), a2s_sem.at[0], a2r_sem.at[src], re, pb).wait_recv()

    each(7, wait_a2)
    ra2[pl.ds(pl.multiple_of(y * 48, 8), 48), :] = ra1[pl.ds(pl.multiple_of(y * 48, 8), 48), :]
    total = ra2[0:48, :]
    for source in range(1, 8):
        total = total + ra2[source * 48 : source * 48 + 48, :]
    padded = jnp.concatenate(
        [dot3(split(total), rotation, NN), jnp.zeros((80, 128), f32)], axis=0
    )
    rotated = padded.T
    for ac in range(4):
        a3s[pl.ds(ac, 32, stride=4), :] = rotated[ac * 32 : ac * 32 + 32]

    def tile(ref, index):
        return ref.at[pl.ds(pl.multiple_of(index * 8, 8), 8), :]

    def a3(d):
        to = (re + d + 1) % 16
        return remote(tile(a3s, to), tile(a3r, re), a3s_sem.at[d], a3r_sem.at[re], to, pb)

    for d in NEAR_RE:
        a3(d).start()
    own_tile = pl.ds(pl.multiple_of(re * 8, 8), 8)
    a3r[own_tile, :] = a3s[own_tile, :]

    def wait_u1x(d):
        src = (x + d + 1) % 4
        remote(x_rows(src), x_rows(src), u1xs.at[0], u1xr.at[src], re, src * 8 + z).wait_recv()

    each(3, wait_u1x)

    def choose(i):
        k, q = i // 4, pb * 4 + i % 4
        index = (
            ((kco[0, k] + qco[0, q]) & 7) * 8 + ((kco[1, k] + qco[1, q]) & 7)
        ) * 8 + ((kco[2, k] + qco[2, q]) & 7)
        sel[pl.ds(i, 1), :] = table[pl.ds(index, 1), :]

    each(32, choose)

    def q_block(src):
        return usq.at[pl.ds(pl.multiple_of(src * 32, 8), 32), :]

    def uq(d):
        to = ((y + d + 1) % 8) * 2 + core
        return remote(sel, q_block(re), uqs.at[d], uqr.at[y], to, pb)

    usq[pl.ds(pl.multiple_of(re * 32, 8), 32), :] = sel[...]

    def uf(i):
        src = i * 2 + core
        return remote(q_block(src), q_block(src), ufs.at[i], ufr.at[i], y * 2 + (1 - core), pb)

    def wait_a3(d):
        src = (re + d + 1) % 16
        remote(tile(a3r, src), tile(a3r, src), a3s_sem.at[0], a3r_sem.at[src], src, pb).wait_recv()

    each(15, wait_a3)

    lane8 = iota((8, 128), 1)
    home = pl.multiple_of(pb * 48, 8)
    for n in range(2):
        v = [
            a3r[pl.ds(n * 4 + ac, 8, stride=16), :]
            + pltpu.roll(a3r[pl.ds(8 + n * 4 + ac, 8, stride=16), :], 48, 1)
            for ac in range(4)
        ]
        r1, r2, r3 = pltpu.roll(v[1], 96, 1), pltpu.roll(v[2], 64, 1), pltpu.roll(v[3], 32, 1)
        thirds = [
            jnp.where(lane8 < 96, v[0], r1),
            jnp.where(lane8 < 64, r1, r2),
            jnp.where(lane8 < 32, r2, r3),
        ]
        for t in range(3):
            for kh in range(2):
                xs[pl.ds(home + kh * 24 + t * 8 + n * 4, 4), :] = thirds[t][kh * 4 : kh * 4 + 4]

    def chunk(src, kh):
        return xs.at[pl.ds(pl.multiple_of(src * 48 + kh * 24, 8), 24), :]

    def bx(kh, zs, d):
        src = x * 8 + zs
        return remote(
            chunk(src, kh), chunk(src, kh), bxs.at[kh * 24 + zs * 3 + d], bxr.at[kh * 32 + src],
            re, ((x + d + 1) % 4) * 8 + z,
        )

    def bz(kh, d):
        return remote(
            chunk(pb, kh), chunk(pb, kh), bzs.at[kh * 7 + d], bzr.at[kh * 8 + z],
            re, x * 8 + (z + d + 1) % 8,
        )

    for kh in range(2):
        for d in NEAR:
            bz(kh, d).start()
        for d in NEAR_X:
            bx(kh, z, d).start()
    for d in NEAR:
        uq(d).start()

    for kh in range(2):
        def pass_on(d):
            zs = (z + d + 1) % 8
            here = chunk(x * 8 + zs, kh)
            remote(here, here, bzs.at[0], bzr.at[kh * 8 + zs], re, pb).wait_recv()
            for e in NEAR_X:
                bx(kh, zs, e).start()

        for d in NEAR:
            pass_on(d)

    uf_own = uf(y)
    uf_own.start()

    def wait_uq(d):
        src = (y + d + 1) % 8
        here = q_block(src * 2 + core)
        remote(here, here, uqs.at[0], uqr.at[src], re, pb).wait_recv()
        uf(src).start()

    for d in NEAR:
        wait_uq(d)

    def wait_uf(i):
        here = q_block(i * 2 + (1 - core))
        remote(here, here, ufs.at[0], ufr.at[i], re, pb).wait_recv()

    each(8, wait_uf)

    def pair_matrices(kk):
        for q in range(4):
            for kl in range(2):
                value = unfold(
                    usq[pl.ds((2 * kk + kl) * 4 + q, 16, stride=32), :], wide, q * 2 + kl
                )
                for part in range(2):
                    for n in range(2):
                        kept = jnp.where(
                            group == 2 * kl + n, value[part * 32 : part * 32 + 32], 0.0
                        )
                        high, low = split(kept)
                        base = pl.multiple_of(
                            (kk * 4 + q) * 256 + part * 128 + kl * 64 + n * 32, 32
                        )
                        bh[pl.ds(base, 32), :] = high
                        bl[pl.ds(base, 32), :] = low

    each(4, pair_matrices)

    group24 = iota((24, 128), 1) >> 5
    row96 = iota((96, 128), 0)
    first = (
        (row96 < 12)
        | ((row96 >= 24) & (row96 < 36))
        | ((row96 >= 48) & (row96 < 60))
        | ((row96 >= 72) & (row96 < 84))
    )
    for kh in range(2):
        def wait_bx(i):
            src = ((x + i // 8 + 1) % 4) * 8 + i % 8
            here = chunk(src, kh)
            remote(here, here, bxs.at[0], bxr.at[kh * 32 + src], re, pb).wait_recv()

        each(24, wait_bx)

        for k4 in range(4):
            for n in range(2):
                for t in range(3):
                    high, low = split(xs[pl.ds(kh * 24 + t * 8 + n * 4 + k4, 32, stride=48), :])
                    to = k4 * 64 + n * 32
                    xh[to : to + 32, t * 128 : t * 128 + 128] = high
                    xl[to : to + 32, t * 128 : t * 128 + 128] = low
        result = dot3((fh[...], fl[...]), (xh[...], xl[...]), NT)
        ys[0:384, :] = result[:, 0:128]
        ys[384:768, :] = result[:, 128:256]

        def finish(kk):
            for q in range(4):
                value = ys[pl.ds(pl.multiple_of(kk * 384 + q * 96, 8), 96), :]
                other = jnp.where(first, pltpu.roll(value, 84, 0), -pltpu.roll(value, 12, 0))
                left = split(jnp.concatenate([value, other], axis=1))
                where = pl.ds(pl.multiple_of(((kh * 2 + kk) * 4 + q) * 256, 256), 256)
                res = dot3(left, (bh[where, :], bl[where, :]), NN)
                quarter = [res[j * 24 : j * 24 + 24] for j in range(4)]
                for kl in range(2):
                    for n in range(2):
                        to = 2 * kl + n
                        mixed = quarter[to]
                        for j in range(4):
                            if j != to:
                                shift = 32 * ((j - to) % 4)
                                mixed = jnp.where(
                                    group24 == j, pltpu.roll(quarter[j], shift, 1), mixed
                                )
                        k = kh * 4 + kk * 2 + kl
                        out[pl.ds((k * 4 + q) * 48 + n, 24, stride=2), :] = mixed

        each(2, finish)

    each(7, lambda d: u1z(d).wait_send())
    each(3, lambda d: u1x(d).wait_send())
    a1.wait_send()
    each(7, lambda d: a2(d).wait_send())
    each(7, lambda d: kz_copy(d).wait_send())
    each(3, lambda d: kx_copy(d).wait_send())
    each(7, lambda d: uq(d).wait_send())
    each(8, lambda d: uf(d).wait_send())
    each(15, lambda d: a3(d).wait_send())
    for kh in range(2):
        each(7, lambda d: bz(kh, d).wait_send())
        each(24, lambda i: bx(kh, i // 3, i % 3).wait_send())


def body(
    wannier_coupling,
    electron_cells,
    phonon_cells,
    kpoint_coords,
    qpoint_coords,
    band_rotations,
    mode_vectors,
):
    hbm = pl.BlockSpec(memory_space=pltpu.HBM)
    vmem = pl.BlockSpec(memory_space=pltpu.VMEM)
    V, S, D = pltpu.VMEM, pltpu.SMEM, pltpu.SemaphoreType.DMA
    result = pl.pallas_call(
        kernel,
        out_shape=pltpu.VMEM((1536, 128), f32),
        in_specs=[hbm] * 7,
        out_specs=vmem,
        scratch_shapes=[
            V((3, 32), i32),
            S((3, 4), i32),
            S((3, 8), i32),
            S((3, 128), i32),
            V((4, 4608), f32),
            V((144, 128), f32),
            V((256, 128), f32),
            V((3072, 128), f32),
            V((768, 128), f32),
            V((384, 128), f32),
            V((384, 128), f32),
            V((512, 128), f32),
            V((32, 128), f32),
            V((128, 128), f32),
            V((64, 128), f32),
            V((512, 128), f32),
            V((512, 128), f32),
            V((128, 128), f32),
            V((128, 128), f32),
            V((1536, 128), f32),
            V((384, 128), f32),
            V((384, 384), bf16),
            V((384, 384), bf16),
            V((4096, 128), bf16),
            V((4096, 128), bf16),
            V((256, 384), bf16),
            V((256, 384), bf16),
            V((768, 128), f32),
            D((1,)), D((16,)), D((5,)),
            D((7,)), D((8,)), D((3,)), D((4,)), D((1,)), D((1,)),
            D((7,)), D((8,)),
            D((7,)), D((8,)), D((3,)), D((4,)), D((7,)), D((8,)), D((8,)), D((8,)),
            D((15,)), D((16,)), D((14,)), D((16,)), D((48,)), D((64,)),
        ],
        compiler_params=pltpu.CompilerParams(
            collective_id=0, has_side_effects=True, vmem_limit_bytes=58 * 1024 * 1024
        ),
        name="interpolate",
    )(
        wannier_coupling.reshape(3072, 128),
        electron_cells,
        phonon_cells,
        kpoint_coords,
        qpoint_coords,
        band_rotations,
        mode_vectors,
    )
    return result.reshape(8, 4, 24, 2, 128).transpose(0, 1, 3, 2, 4).reshape(8, 4, 2, 3072)


def solution(mesh):
    return jax.shard_map(
        body,
        mesh=mesh,
        in_specs=(
            P("re", None, "pb", None),
            P(None, "re"),
            P(),
            P(),
            P(),
            P("pb", None),
            P("pb", None),
        ),
        out_specs=P(None, "pb", "re", None),
        check_vma=False,
    )
```

```python
import math

import jax
import jax.numpy as jnp
from jax import lax
from jax.experimental import pallas as pl
from jax.experimental.pallas import tpu as pltpu
from jax.sharding import PartitionSpec as P

f32, bf16, i32 = jnp.float32, jnp.bfloat16, jnp.int32
MESH = pl.DeviceIdType.MESH
NEAR = (0, 6, 1, 5, 2, 4, 3)
FAR = NEAR[::-1]
NEAR_X = (0, 2, 1)
NN = ((1,), (0,))
NT = ((1,), (1,))


def split(value):
    high = value.astype(bf16)
    return high, (value - high.astype(f32)).astype(bf16)


def dot(left, right, dims):
    return lax.dot_general(left, right, (dims, ((), ())), preferred_element_type=f32)


def dot3(left, right, dims):
    return (
        dot(left[0], right[0], dims) + dot(left[1], right[0], dims) + dot(left[0], right[1], dims)
    )


def iota(shape, axis):
    return lax.broadcasted_iota(i32, shape, axis)


def wave(turns, period):
    cosine = jnp.zeros(turns.shape, f32)
    sine = jnp.zeros(turns.shape, f32)
    for step in range(period):
        hit = turns == step
        angle = 2 * math.pi * step / period
        cosine = jnp.where(hit, jnp.float32(math.cos(angle)), cosine)
        sine = jnp.where(hit, jnp.float32(math.sin(angle)), sine)
    return cosine, sine


def unfold(slices, wide, region):
    group = iota((16, 128), 1) >> 5
    for j in range(4):
        wide[pl.ds(region * 64 + j, 16, stride=4), :] = jnp.where(group == j, slices, 0.0)
    kept = wide[region * 64 : region * 64 + 64, :]
    kept = kept + pltpu.roll(kept, 64, 1)
    return kept + pltpu.roll(kept, 32, 1)


def kernel(
    g_hbm, cells_hbm, pcell_hbm, kco_hbm, qco_hbm, rot_hbm, modes_hbm, out,
    cells, pcell, kco, qco, flat, modes, rot, g, acc, ra1, ra2, table, sel, kz, kx, usq, wide,
    ga, turned_rows, a3s, a3r, xs, fq, fh, fl, bh, bl, xh, xl, ys,
    gsem, rotsem, insem, u1zs, u1zr, u1xs, u1xr, a1s_sem, a1r_sem, a2s_sem, a2r_sem,
    kzs, kzr, kxs, kxr, uqs, uqr, ufs, ufr, a4s_sem, a4r_sem, a3s_sem, a3r_sem, bzs, bzr, bxs, bxr,
):
    re = lax.axis_index("re")
    pb = lax.axis_index("pb")
    y, core = re // 2, re % 2
    x, z = pb // 8, pb % 8

    def remote(src, dst, ssem, rsem, to_re, to_pb):
        return pltpu.make_async_remote_copy(
            src_ref=src, dst_ref=dst, send_sem=ssem, recv_sem=rsem,
            device_id=(to_re, to_pb), device_id_type=MESH,
        )

    def each(count, body):
        def step(i, carry):
            body(i)
            return carry

        lax.fori_loop(0, count, step, 0)

    barrier = pltpu.get_barrier_semaphore()

    def greet_y(d):
        pl.semaphore_signal(
            barrier, 1, device_id=(((y + d + 1) % 8) * 2 + core, pb), device_id_type=MESH
        )

    def greet_z(d):
        pl.semaphore_signal(
            barrier, 1, device_id=(re, x * 8 + (z + d + 1) % 8), device_id_type=MESH
        )

    def greet_x(d):
        pl.semaphore_signal(
            barrier, 1, device_id=(re, ((x + d + 1) % 4) * 8 + z), device_id_type=MESH
        )

    for d in NEAR[::-1]:
        greet_y(d)
        greet_z(d)
    each(3, greet_x)
    pl.semaphore_signal(barrier, 1, device_id=(y * 2 + (1 - core), pb), device_id_type=MESH)
    small = [
        pltpu.make_async_copy(src, dst, insem.at[i])
        for i, (src, dst) in enumerate(
            [(kco_hbm, kco), (cells_hbm, cells), (pcell_hbm, pcell), (qco_hbm, qco)]
        )
    ]
    modes_copy = pltpu.make_async_copy(modes_hbm, flat, insem.at[4])

    def rot_copy(i):
        return pltpu.make_async_copy(
            rot_hbm.at[:, pl.ds(pl.multiple_of(i * 128, 128), 128)],
            rot.at[pl.ds(pl.multiple_of(i * 16, 16), 16), :],
            rotsem.at[i],
        )

    g_copy = pltpu.make_async_copy(g_hbm, g, gsem.at[0])
    g_copy.start()
    for copy in small:
        copy.start()
    each(16, lambda i: rot_copy(i).start())
    own_rows = table.at[pl.ds(pl.multiple_of(pb * 16, 16), 16), :]
    modes_copy.start()

    for copy in small:
        copy.wait()

    row = iota((8, 64), 0)
    turns = jnp.zeros((8, 64), i32)
    twice = jnp.concatenate([cells[...], cells[...]], axis=1)
    for d in range(3):
        coef = jnp.zeros((8, 64), i32)
        for k in range(8):
            coef = jnp.where(row == k, 2 * kco[d, k] + 1, coef)
        turns = turns + coef * jnp.broadcast_to(twice[d : d + 1, :], (8, 64))
    cosine, sine = wave(turns & 15, 16)
    waves = jnp.concatenate(split(jnp.concatenate([cosine, sine], axis=0)), axis=0)

    k_index = ((kco[0, y] & 7) * 8 + (kco[1, y] & 7)) * 8 + (kco[2, y] & 7)
    each(16, lambda i: rot_copy(i).wait())
    held = jnp.full((16, 128), k_index >> 4, i32) == jnp.full((16, 128), pb, i32)

    def kz_block(src):
        return kz.at[pl.ds(pl.multiple_of(src * 16, 16), 16), :]

    def kx_block(src):
        return kx.at[pl.ds(pl.multiple_of(src * 16, 16), 16), :]

    kz[pl.ds(pl.multiple_of(z * 16, 16), 16), :] = jnp.where(
        held, rot[pl.ds(k_index & 15, 16, stride=16), :], 0.0
    )
    own_rows[...] = rot[pl.ds(pl.multiple_of(re * 16, 16), 16), :]

    odd = ((iota((8, 128), 1) >> 5) & 1) == 1

    def phase_part(half, pp):
        for i in range(12):
            highs, lows = [], []
            for lo in range(2):
                start = half * 48 + pp * 24 + 2 * i + lo
                high, low = split(g[pl.ds(start, 32, stride=96), :])
                highs.append(high)
                lows.append(low)
            stacked = jnp.concatenate(
                [jnp.concatenate(highs, axis=1), jnp.concatenate(lows, axis=1)], axis=0
            )
            both = dot(waves, stacked, NN)
            both = both[0:16] + both[16:32]
            for lo in range(2):
                real = both[0:8, lo * 128 : lo * 128 + 128]
                turned = both[8:16, lo * 128 : lo * 128 + 128]
                swapped = jnp.where(odd, pltpu.roll(turned, 32, 1), -pltpu.roll(turned, 96, 1))
                acc[pl.ds(half * 384 + pp * 24 + lo * 12 + i, 8, stride=48), :] = real + swapped

    g_copy.wait()
    for pp in range(2):
        phase_part(1 - core, pp)
    for pp in range(2):
        phase_part(core, pp)
    pl.semaphore_wait(barrier, 18)
    a1 = remote(
        acc.at[pl.ds(pl.multiple_of((1 - core) * 384, 8), 384), :], ra1,
        a1s_sem.at[0], a1r_sem.at[0], y * 2 + (1 - core), pb,
    )
    a1.start()

    def kz_copy(d):
        return remote(
            kz_block(z), kz_block(z), kzs.at[d], kzr.at[z], re, x * 8 + (z + d + 1) % 8
        )

    def u1z(d):
        return remote(
            own_rows, own_rows, u1zs.at[d], u1zr.at[z], re, x * 8 + (z + d + 1) % 8
        )

    for d in FAR:
        kz_copy(d).start()

    a1.wait_recv()
    mine = pl.multiple_of(core * 384, 8)
    ra1[...] = ra1[...] + acc[pl.ds(mine, 384), :]

    def block(ref, index):
        return ref.at[pl.ds(pl.multiple_of(index * 48, 8), 48), :]

    def a2(d):
        to = (y + d + 1) % 8
        return remote(block(ra1, to), block(ra2, y), a2s_sem.at[d], a2r_sem.at[y], to * 2 + core, pb)

    for d in FAR:
        a2(d).start()
    for d in NEAR:
        u1z(d).start()

    def wait_kz(d):
        src = (z + d + 1) % 8
        remote(kz_block(src), kz_block(src), kzs.at[0], kzr.at[src], re, pb).wait_recv()

    each(7, wait_kz)
    found = kz[0:16, :]
    for s in range(1, 8):
        found = found + kz[s * 16 : s * 16 + 16, :]
    kx[pl.ds(pl.multiple_of(x * 16, 16), 16), :] = found

    def kx_copy(d):
        return remote(
            kx_block(x), kx_block(x), kxs.at[d], kxr.at[x], re, ((x + d + 1) % 4) * 8 + z
        )

    each(3, lambda d: kx_copy(d).start())

    def z_rows(src):
        return table.at[pl.ds(pl.multiple_of((x * 8 + src) * 16, 16), 16), :]

    def wait_u1z(d):
        src = (z + d + 1) % 8
        remote(z_rows(src), z_rows(src), u1zs.at[0], u1zr.at[src], re, x * 8 + src).wait_recv()

    each(7, wait_u1z)

    def x_rows(src):
        return table.at[pl.ds(pl.multiple_of(src * 128, 128), 128), :]

    def u1x(d):
        return remote(x_rows(x), x_rows(x), u1xs.at[d], u1xr.at[x], re, ((x + d + 1) % 4) * 8 + z)

    each(3, lambda d: u1x(d).start())

    modes_copy.wait()
    for tile_index in range(36):
        modes[tile_index * 4 : tile_index * 4 + 4, :] = flat[
            :, tile_index * 128 : tile_index * 128 + 128
        ]
    lane12 = iota((12, 128), 1)
    permute_row = iota((96, 128), 0)
    block24 = (
        (permute_row >= 24).astype(i32)
        + (permute_row >= 48).astype(i32)
        + (permute_row >= 72).astype(i32)
    )
    rest = permute_row - 24 * block24
    part = (rest >= 12).astype(i32)
    target = part * 48 + 4 * (rest - 12 * part) + block24
    permute = (iota((96, 128), 1) == target).astype(f32).astype(bf16)

    def mode_q(q):
        v = [modes[pl.ds(tt * 4 + q, 12, stride=12), :] for tt in range(3)]
        r0, r1, r2 = pltpu.roll(v[0], 32, 1), pltpu.roll(v[1], 32, 1), pltpu.roll(v[1], 64, 1)
        r3, r4 = pltpu.roll(v[2], 64, 1), pltpu.roll(v[2], 96, 1)
        raw = [
            v[0],
            jnp.where(lane12 < 32, r0, r1),
            jnp.where(lane12 < 64, r2, r3),
            r4,
        ]
        plain, crossed = [], []
        for value in raw:
            value = jnp.where(lane12 < 96, value, 0.0)
            other = jnp.where(lane12 < 48, -pltpu.roll(value, 80, 1), pltpu.roll(value, 48, 1))
            plain.append(value)
            crossed.append(jnp.where(lane12 < 96, other, 0.0))
        point = pb * 4 + q
        for p in range(4):
            turn = (
                qco[0, point] * pcell[0, p]
                + qco[1, point] * pcell[1, p]
                + qco[2, point] * pcell[2, p]
            ) & 7
            cos_p, sin_p = wave(jnp.full((1, 128), turn, i32), 8)
            for a2 in range(2):
                for lo in range(2):
                    i = 2 * lo + a2
                    base = a2 * 192 + p * 24 + lo * 12
                    fq[base : base + 12, :] = cos_p * plain[i] + sin_p * crossed[i]
                    fq[base + 96 : base + 108, :] = cos_p * crossed[i] - sin_p * plain[i]
        high, low = split(fq[...])
        where = pl.ds(pl.multiple_of(q * 96, 96), 96)
        fh[where, :] = dot(permute, high, NT).astype(bf16)
        fl[where, :] = dot(permute, low, NT).astype(bf16)

    each(4, mode_q)

    def wait_kx(d):
        src = (x + d + 1) % 4
        remote(kx_block(src), kx_block(src), kxs.at[0], kxr.at[src], re, pb).wait_recv()

    each(3, wait_kx)
    k_row = kx[0:16, :] + kx[16:32, :] + kx[32:48, :] + kx[48:64, :]
    turned = unfold(k_row, wide, 0)
    real, imag = turned[0:32], turned[32:64]
    group = iota((32, 128), 1) >> 5
    pieces = []
    for a in range(2):
        pieces.append(jnp.where(group == 2 * a, real, jnp.where(group == 2 * a + 1, imag, 0.0)))
        pieces.append(jnp.where(group == 2 * a, -imag, jnp.where(group == 2 * a + 1, real, 0.0)))
    rotation = split(jnp.concatenate(pieces, axis=0))

    def wait_a2(d):
        src = (y + d + 1) % 8
        remote(block(ra2, src), block(ra2, src), a2s_sem.at[0], a2r_sem.at[src], re, pb).wait_recv()

    each(7, wait_a2)
    ra2[pl.ds(pl.multiple_of(y * 48, 8), 48), :] = ra1[pl.ds(pl.multiple_of(y * 48, 8), 48), :]
    total = ra2[0:48, :]
    for source in range(1, 8):
        total = total + ra2[source * 48 : source * 48 + 48, :]
    def half_of(which):
        return ga.at[pl.ds(pl.multiple_of(which * 48, 8), 48), :]

    half_of(core)[...] = total
    a4 = remote(
        half_of(core), half_of(core), a4s_sem.at[0], a4r_sem.at[0], y * 2 + (1 - core), pb
    )
    a4.start()
    a4.wait_recv()
    padded = jnp.concatenate(
        [dot3(split(ga[...]), rotation, NN), jnp.zeros((32, 128), f32)], axis=0
    )
    turned_rows[...] = padded.T
    for n in range(2):
        for ac in range(4):
            a3s[pl.ds(n * 4 + ac, 8, stride=8), :] = turned_rows[
                pl.ds(ac * 32 + 2 * core + n, 8, stride=4), :
            ]

    def tile(ref, index):
        return ref.at[pl.ds(pl.multiple_of(index * 8, 8), 8), :]

    def a3(d):
        to = (y + d + 1) % 8
        return remote(
            tile(a3s, to), tile(a3r, y), a3s_sem.at[d], a3r_sem.at[y], to * 2 + core, pb
        )

    for d in FAR:
        a3(d).start()
    own_tile = pl.ds(pl.multiple_of(y * 8, 8), 8)
    a3r[own_tile, :] = a3s[own_tile, :]

    def wait_u1x(d):
        src = (x + d + 1) % 4
        remote(x_rows(src), x_rows(src), u1xs.at[0], u1xr.at[src], re, src * 8 + z).wait_recv()

    each(3, wait_u1x)

    def choose(i):
        k, q = i // 4, pb * 4 + i % 4
        index = (
            ((kco[0, k] + qco[0, q]) & 7) * 8 + ((kco[1, k] + qco[1, q]) & 7)
        ) * 8 + ((kco[2, k] + qco[2, q]) & 7)
        sel[pl.ds(i, 1), :] = table[pl.ds(index, 1), :]

    each(32, choose)

    def q_block(src):
        return usq.at[pl.ds(pl.multiple_of(src * 32, 8), 32), :]

    def uq(d):
        to = ((y + d + 1) % 8) * 2 + core
        return remote(sel, q_block(re), uqs.at[d], uqr.at[y], to, pb)

    usq[pl.ds(pl.multiple_of(re * 32, 8), 32), :] = sel[...]

    def uf(i):
        src = i * 2 + core
        return remote(q_block(src), q_block(src), ufs.at[i], ufr.at[i], y * 2 + (1 - core), pb)

    def wait_a3(d):
        src = (y + d + 1) % 8
        remote(tile(a3r, src), tile(a3r, src), a3s_sem.at[0], a3r_sem.at[src], re, pb).wait_recv()

    each(7, wait_a3)

    lane8 = iota((8, 128), 1)
    home = pl.multiple_of(pb * 48, 8)
    for n in range(2):
        v = [
            a3r[pl.ds(n * 4 + ac, 8, stride=8), :]
            for ac in range(4)
        ]
        r1, r2, r3 = pltpu.roll(v[1], 96, 1), pltpu.roll(v[2], 64, 1), pltpu.roll(v[3], 32, 1)
        thirds = [
            jnp.where(lane8 < 96, v[0], r1),
            jnp.where(lane8 < 64, r1, r2),
            jnp.where(lane8 < 32, r2, r3),
        ]
        for t in range(3):
            for kh in range(2):
                xs[pl.ds(home + kh * 24 + t * 8 + n * 4, 4), :] = thirds[t][kh * 4 : kh * 4 + 4]

    def chunk(src, kh):
        return xs.at[pl.ds(pl.multiple_of(src * 48 + kh * 24, 8), 24), :]

    def bx(kh, zs, d):
        src = x * 8 + zs
        return remote(
            chunk(src, kh), chunk(src, kh), bxs.at[kh * 24 + zs * 3 + d], bxr.at[kh * 32 + src],
            re, ((x + d + 1) % 4) * 8 + z,
        )

    def bz(kh, d):
        return remote(
            chunk(pb, kh), chunk(pb, kh), bzs.at[kh * 7 + d], bzr.at[kh * 8 + z],
            re, x * 8 + (z + d + 1) % 8,
        )

    for kh in range(2):
        for d in NEAR:
            bz(kh, d).start()
        for d in NEAR_X:
            bx(kh, z, d).start()
    for d in NEAR:
        uq(d).start()

    for kh in range(2):
        def pass_on(d):
            zs = (z + d + 1) % 8
            here = chunk(x * 8 + zs, kh)
            remote(here, here, bzs.at[0], bzr.at[kh * 8 + zs], re, pb).wait_recv()
            for e in NEAR_X:
                bx(kh, zs, e).start()

        for d in NEAR:
            pass_on(d)

    uf_own = uf(y)
    uf_own.start()

    def wait_uq(d):
        src = (y + d + 1) % 8
        here = q_block(src * 2 + core)
        remote(here, here, uqs.at[0], uqr.at[src], re, pb).wait_recv()
        uf(src).start()

    for d in NEAR:
        wait_uq(d)

    def wait_uf(i):
        here = q_block(i * 2 + (1 - core))
        remote(here, here, ufs.at[0], ufr.at[i], re, pb).wait_recv()

    each(8, wait_uf)

    def pair_matrices(kk):
        for q in range(4):
            for kl in range(2):
                value = unfold(
                    usq[pl.ds((2 * kk + kl) * 4 + q, 16, stride=32), :], wide, q * 2 + kl
                )
                for part in range(2):
                    for n in range(2):
                        kept = jnp.where(
                            group == 2 * kl + n, value[part * 32 : part * 32 + 32], 0.0
                        )
                        high, low = split(kept)
                        base = pl.multiple_of(
                            (kk * 4 + q) * 256 + part * 128 + kl * 64 + n * 32, 32
                        )
                        bh[pl.ds(base, 32), :] = high
                        bl[pl.ds(base, 32), :] = low

    each(4, pair_matrices)

    group24 = iota((24, 128), 1) >> 5
    row96 = iota((96, 128), 0)
    first = (
        (row96 < 12)
        | ((row96 >= 24) & (row96 < 36))
        | ((row96 >= 48) & (row96 < 60))
        | ((row96 >= 72) & (row96 < 84))
    )
    for kh in range(2):
        def wait_bx(i):
            src = ((x + i // 8 + 1) % 4) * 8 + i % 8
            here = chunk(src, kh)
            remote(here, here, bxs.at[0], bxr.at[kh * 32 + src], re, pb).wait_recv()

        each(24, wait_bx)

        for k4 in range(4):
            for n in range(2):
                for t in range(3):
                    high, low = split(xs[pl.ds(kh * 24 + t * 8 + n * 4 + k4, 32, stride=48), :])
                    to = k4 * 64 + n * 32
                    xh[to : to + 32, t * 128 : t * 128 + 128] = high
                    xl[to : to + 32, t * 128 : t * 128 + 128] = low
        result = dot3((fh[...], fl[...]), (xh[...], xl[...]), NT)
        ys[0:384, :] = result[:, 0:128]
        ys[384:768, :] = result[:, 128:256]

        def finish(kk):
            for q in range(4):
                value = ys[pl.ds(pl.multiple_of(kk * 384 + q * 96, 8), 96), :]
                other = jnp.where(first, pltpu.roll(value, 84, 0), -pltpu.roll(value, 12, 0))
                left = split(jnp.concatenate([value, other], axis=1))
                where = pl.ds(pl.multiple_of(((kh * 2 + kk) * 4 + q) * 256, 256), 256)
                res = dot3(left, (bh[where, :], bl[where, :]), NN)
                quarter = [res[j * 24 : j * 24 + 24] for j in range(4)]
                for kl in range(2):
                    for n in range(2):
                        to = 2 * kl + n
                        mixed = quarter[to]
                        for j in range(4):
                            if j != to:
                                shift = 32 * ((j - to) % 4)
                                mixed = jnp.where(
                                    group24 == j, pltpu.roll(quarter[j], shift, 1), mixed
                                )
                        k = kh * 4 + kk * 2 + kl
                        out[pl.ds((k * 4 + q) * 48 + n, 24, stride=2), :] = mixed

        each(2, finish)

    each(7, lambda d: u1z(d).wait_send())
    each(3, lambda d: u1x(d).wait_send())
    a1.wait_send()
    each(7, lambda d: a2(d).wait_send())
    each(7, lambda d: kz_copy(d).wait_send())
    each(3, lambda d: kx_copy(d).wait_send())
    each(7, lambda d: uq(d).wait_send())
    each(8, lambda d: uf(d).wait_send())
    a4.wait_send()
    each(7, lambda d: a3(d).wait_send())
    for kh in range(2):
        each(7, lambda d: bz(kh, d).wait_send())
        each(24, lambda i: bx(kh, i // 3, i % 3).wait_send())


def body(
    wannier_coupling,
    electron_cells,
    phonon_cells,
    kpoint_coords,
    qpoint_coords,
    band_rotations,
    mode_vectors,
):
    hbm = pl.BlockSpec(memory_space=pltpu.HBM)
    vmem = pl.BlockSpec(memory_space=pltpu.VMEM)
    V, S, D = pltpu.VMEM, pltpu.SMEM, pltpu.SemaphoreType.DMA
    result = pl.pallas_call(
        kernel,
        out_shape=pltpu.VMEM((1536, 128), f32),
        in_specs=[hbm] * 7,
        out_specs=vmem,
        scratch_shapes=[
            V((3, 32), i32),
            S((3, 4), i32),
            S((3, 8), i32),
            S((3, 128), i32),
            V((4, 4608), f32),
            V((144, 128), f32),
            V((256, 128), f32),
            V((3072, 128), f32),
            V((768, 128), f32),
            V((384, 128), f32),
            V((384, 128), f32),
            V((512, 128), f32),
            V((32, 128), f32),
            V((128, 128), f32),
            V((64, 128), f32),
            V((512, 128), f32),
            V((512, 128), f32),
            V((96, 128), f32),
            V((128, 128), f32),
            V((64, 128), f32),
            V((64, 128), f32),
            V((1536, 128), f32),
            V((384, 128), f32),
            V((384, 384), bf16),
            V((384, 384), bf16),
            V((4096, 128), bf16),
            V((4096, 128), bf16),
            V((256, 384), bf16),
            V((256, 384), bf16),
            V((768, 128), f32),
            D((1,)), D((16,)), D((5,)),
            D((7,)), D((8,)), D((3,)), D((4,)), D((1,)), D((1,)),
            D((7,)), D((8,)),
            D((7,)), D((8,)), D((3,)), D((4,)), D((7,)), D((8,)), D((8,)), D((8,)),
            D((1,)), D((1,)), D((7,)), D((8,)), D((14,)), D((16,)), D((48,)), D((64,)),
        ],
        compiler_params=pltpu.CompilerParams(
            collective_id=0, has_side_effects=True, vmem_limit_bytes=58 * 1024 * 1024
        ),
        name="interpolate",
    )(
        wannier_coupling.reshape(3072, 128),
        electron_cells,
        phonon_cells,
        kpoint_coords,
        qpoint_coords,
        band_rotations,
        mode_vectors,
    )
    return result.reshape(8, 4, 24, 2, 128).transpose(0, 1, 3, 2, 4).reshape(8, 4, 2, 3072)


def solution(mesh):
    return jax.shard_map(
        body,
        mesh=mesh,
        in_specs=(
            P("re", None, "pb", None),
            P(None, "re"),
            P(),
            P(),
            P(),
            P("pb", None),
            P("pb", None),
        ),
        out_specs=P(None, "pb", "re", None),
        check_vma=False,
    )
```

```python
import math

import jax
import jax.numpy as jnp
from jax import lax
from jax.experimental import pallas as pl
from jax.experimental.pallas import tpu as pltpu
from jax.sharding import PartitionSpec as P

f32, bf16, i32 = jnp.float32, jnp.bfloat16, jnp.int32
MESH = pl.DeviceIdType.MESH
NEAR = (0, 6, 1, 5, 2, 4, 3)
FAR = NEAR[::-1]
NEAR_X = (0, 2, 1)
NN = ((1,), (0,))
NT = ((1,), (1,))


def split(value):
    high = value.astype(bf16)
    return high, (value - high.astype(f32)).astype(bf16)


def dot(left, right, dims):
    return lax.dot_general(left, right, (dims, ((), ())), preferred_element_type=f32)


def dot3(left, right, dims):
    return (
        dot(left[0], right[0], dims) + dot(left[1], right[0], dims) + dot(left[0], right[1], dims)
    )


def iota(shape, axis):
    return lax.broadcasted_iota(i32, shape, axis)


def wave(turns, period):
    cosine = jnp.zeros(turns.shape, f32)
    sine = jnp.zeros(turns.shape, f32)
    for step in range(period):
        hit = turns == step
        angle = 2 * math.pi * step / period
        cosine = jnp.where(hit, jnp.float32(math.cos(angle)), cosine)
        sine = jnp.where(hit, jnp.float32(math.sin(angle)), sine)
    return cosine, sine


def unfold(slices, wide, region):
    group = iota((16, 128), 1) >> 5
    for j in range(4):
        wide[pl.ds(region * 64 + j, 16, stride=4), :] = jnp.where(group == j, slices, 0.0)
    kept = wide[region * 64 : region * 64 + 64, :]
    kept = kept + pltpu.roll(kept, 64, 1)
    return kept + pltpu.roll(kept, 32, 1)


def kernel(
    g_hbm, cells_hbm, pcell_hbm, kco_hbm, qco_hbm, rot_hbm, modes_hbm, out,
    cells, pcell, kco, qco, flat, modes, rot, g, acc, ra1, ra2, table, sel, kz, kx, usq, wide,
    ga, turned_rows, a3s, a3r, xs, fq, fh, fl, bh, bl, xh, xl, ys,
    gsem, rotsem, insem, u1zs, u1zr, u1xs, u1xr, a1s_sem, a1r_sem, a2s_sem, a2r_sem,
    kzs, kzr, kxs, kxr, uqs, uqr, ufs, ufr, a4s_sem, a4r_sem, a3s_sem, a3r_sem, bzs, bzr, bxs, bxr,
):
    re = lax.axis_index("re")
    pb = lax.axis_index("pb")
    y, core = re // 2, re % 2
    x, z = pb // 8, pb % 8

    def remote(src, dst, ssem, rsem, to_re, to_pb):
        return pltpu.make_async_remote_copy(
            src_ref=src, dst_ref=dst, send_sem=ssem, recv_sem=rsem,
            device_id=(to_re, to_pb), device_id_type=MESH,
        )

    def each(count, body):
        def step(i, carry):
            body(i)
            return carry

        lax.fori_loop(0, count, step, 0)

    barrier = pltpu.get_barrier_semaphore()

    def greet_y(d):
        pl.semaphore_signal(
            barrier, 1, device_id=(((y + d + 1) % 8) * 2 + core, pb), device_id_type=MESH
        )

    def greet_z(d):
        pl.semaphore_signal(
            barrier, 1, device_id=(re, x * 8 + (z + d + 1) % 8), device_id_type=MESH
        )

    def greet_x(d):
        pl.semaphore_signal(
            barrier, 1, device_id=(re, ((x + d + 1) % 4) * 8 + z), device_id_type=MESH
        )

    for d in NEAR[::-1]:
        greet_y(d)
        greet_z(d)
    each(3, greet_x)
    pl.semaphore_signal(barrier, 1, device_id=(y * 2 + (1 - core), pb), device_id_type=MESH)
    small = [
        pltpu.make_async_copy(src, dst, insem.at[i])
        for i, (src, dst) in enumerate(
            [(kco_hbm, kco), (cells_hbm, cells), (pcell_hbm, pcell), (qco_hbm, qco)]
        )
    ]
    modes_copy = pltpu.make_async_copy(modes_hbm, flat, insem.at[4])

    def rot_copy(i):
        return pltpu.make_async_copy(
            rot_hbm.at[:, pl.ds(pl.multiple_of(i * 128, 128), 128)],
            rot.at[pl.ds(pl.multiple_of(i * 16, 16), 16), :],
            rotsem.at[i],
        )

    g_copy = pltpu.make_async_copy(g_hbm, g, gsem.at[0])
    g_copy.start()
    for copy in small:
        copy.start()
    each(16, lambda i: rot_copy(i).start())
    own_rows = table.at[pl.ds(pl.multiple_of(pb * 16, 16), 16), :]
    modes_copy.start()

    for copy in small:
        copy.wait()

    row = iota((8, 64), 0)
    turns = jnp.zeros((8, 64), i32)
    twice = jnp.concatenate([cells[...], cells[...]], axis=1)
    for d in range(3):
        coef = jnp.zeros((8, 64), i32)
        for k in range(8):
            coef = jnp.where(row == k, 2 * kco[d, k] + 1, coef)
        turns = turns + coef * jnp.broadcast_to(twice[d : d + 1, :], (8, 64))
    cosine, sine = wave(turns & 15, 16)
    waves = jnp.concatenate(split(jnp.concatenate([cosine, sine], axis=0)), axis=0)

    k_index = ((kco[0, y] & 7) * 8 + (kco[1, y] & 7)) * 8 + (kco[2, y] & 7)
    each(16, lambda i: rot_copy(i).wait())
    held = jnp.full((16, 128), k_index >> 4, i32) == jnp.full((16, 128), pb, i32)

    def kz_block(src):
        return kz.at[pl.ds(pl.multiple_of(src * 16, 16), 16), :]

    def kx_block(src):
        return kx.at[pl.ds(pl.multiple_of(src * 16, 16), 16), :]

    kz[pl.ds(pl.multiple_of(z * 16, 16), 16), :] = jnp.where(
        held, rot[pl.ds(k_index & 15, 16, stride=16), :], 0.0
    )
    own_rows[...] = rot[pl.ds(pl.multiple_of(re * 16, 16), 16), :]

    odd = ((iota((8, 128), 1) >> 5) & 1) == 1

    def phase_part(half, pp):
        for i in range(12):
            highs, lows = [], []
            for lo in range(2):
                start = half * 48 + pp * 24 + 2 * i + lo
                high, low = split(g[pl.ds(start, 32, stride=96), :])
                highs.append(high)
                lows.append(low)
            stacked = jnp.concatenate(
                [jnp.concatenate(highs, axis=1), jnp.concatenate(lows, axis=1)], axis=0
            )
            both = dot(waves, stacked, NN)
            both = both[0:16] + both[16:32]
            for lo in range(2):
                real = both[0:8, lo * 128 : lo * 128 + 128]
                turned = both[8:16, lo * 128 : lo * 128 + 128]
                swapped = jnp.where(odd, pltpu.roll(turned, 32, 1), -pltpu.roll(turned, 96, 1))
                acc[pl.ds(half * 384 + pp * 24 + lo * 12 + i, 8, stride=48), :] = real + swapped

    g_copy.wait()
    for pp in range(2):
        phase_part(1 - core, pp)
    for pp in range(2):
        phase_part(core, pp)
    pl.semaphore_wait(barrier, 18)
    a1 = remote(
        acc.at[pl.ds(pl.multiple_of((1 - core) * 384, 8), 384), :], ra1,
        a1s_sem.at[0], a1r_sem.at[0], y * 2 + (1 - core), pb,
    )
    a1.start()

    def kz_copy(d):
        return remote(
            kz_block(z), kz_block(z), kzs.at[d], kzr.at[z], re, x * 8 + (z + d + 1) % 8
        )

    def u1z(d):
        return remote(
            own_rows, own_rows, u1zs.at[d], u1zr.at[z], re, x * 8 + (z + d + 1) % 8
        )

    for d in FAR:
        kz_copy(d).start()

    a1.wait_recv()
    mine = pl.multiple_of(core * 384, 8)
    ra1[...] = ra1[...] + acc[pl.ds(mine, 384), :]

    def block(ref, index):
        return ref.at[pl.ds(pl.multiple_of(index * 48, 8), 48), :]

    def a2(d):
        to = (y + d + 1) % 8
        return remote(block(ra1, to), block(ra2, y), a2s_sem.at[d], a2r_sem.at[y], to * 2 + core, pb)

    for d in FAR:
        a2(d).start()
    for d in NEAR:
        u1z(d).start()

    def wait_kz(d):
        src = (z + d + 1) % 8
        remote(kz_block(src), kz_block(src), kzs.at[0], kzr.at[src], re, pb).wait_recv()

    each(7, wait_kz)
    found = kz[0:16, :]
    for s in range(1, 8):
        found = found + kz[s * 16 : s * 16 + 16, :]
    kx[pl.ds(pl.multiple_of(x * 16, 16), 16), :] = found

    def kx_copy(d):
        return remote(
            kx_block(x), kx_block(x), kxs.at[d], kxr.at[x], re, ((x + d + 1) % 4) * 8 + z
        )

    each(3, lambda d: kx_copy(d).start())

    def z_rows(src):
        return table.at[pl.ds(pl.multiple_of((x * 8 + src) * 16, 16), 16), :]

    def wait_u1z(d):
        src = (z + d + 1) % 8
        remote(z_rows(src), z_rows(src), u1zs.at[0], u1zr.at[src], re, x * 8 + src).wait_recv()

    each(7, wait_u1z)

    def x_rows(src):
        return table.at[pl.ds(pl.multiple_of(src * 128, 128), 128), :]

    def u1x(d):
        return remote(x_rows(x), x_rows(x), u1xs.at[d], u1xr.at[x], re, ((x + d + 1) % 4) * 8 + z)

    each(3, lambda d: u1x(d).start())

    modes_copy.wait()
    for tile_index in range(36):
        modes[tile_index * 4 : tile_index * 4 + 4, :] = flat[
            :, tile_index * 128 : tile_index * 128 + 128
        ]
    lane12 = iota((12, 128), 1)
    permute_row = iota((96, 128), 0)
    block24 = (
        (permute_row >= 24).astype(i32)
        + (permute_row >= 48).astype(i32)
        + (permute_row >= 72).astype(i32)
    )
    rest = permute_row - 24 * block24
    part = (rest >= 12).astype(i32)
    target = part * 48 + 4 * (rest - 12 * part) + block24
    permute = (iota((96, 128), 1) == target).astype(f32).astype(bf16)

    def mode_q(q):
        v = [modes[pl.ds(tt * 4 + q, 12, stride=12), :] for tt in range(3)]
        r0, r1, r2 = pltpu.roll(v[0], 32, 1), pltpu.roll(v[1], 32, 1), pltpu.roll(v[1], 64, 1)
        r3, r4 = pltpu.roll(v[2], 64, 1), pltpu.roll(v[2], 96, 1)
        raw = [
            v[0],
            jnp.where(lane12 < 32, r0, r1),
            jnp.where(lane12 < 64, r2, r3),
            r4,
        ]
        plain, crossed = [], []
        for value in raw:
            value = jnp.where(lane12 < 96, value, 0.0)
            other = jnp.where(lane12 < 48, -pltpu.roll(value, 80, 1), pltpu.roll(value, 48, 1))
            plain.append(value)
            crossed.append(jnp.where(lane12 < 96, other, 0.0))
        point = pb * 4 + q
        for p in range(4):
            turn = (
                qco[0, point] * pcell[0, p]
                + qco[1, point] * pcell[1, p]
                + qco[2, point] * pcell[2, p]
            ) & 7
            cos_p, sin_p = wave(jnp.full((1, 128), turn, i32), 8)
            for a2 in range(2):
                for lo in range(2):
                    i = 2 * lo + a2
                    base = a2 * 192 + p * 24 + lo * 12
                    fq[base : base + 12, :] = cos_p * plain[i] + sin_p * crossed[i]
                    fq[base + 96 : base + 108, :] = cos_p * crossed[i] - sin_p * plain[i]
        high, low = split(fq[0:384, :])
        where = pl.ds(pl.multiple_of(q * 96, 96), 96)
        fh[where, :] = dot(permute, high, NT).astype(bf16)
        fl[where, :] = dot(permute, low, NT).astype(bf16)

    each(4, mode_q)

    def wait_kx(d):
        src = (x + d + 1) % 4
        remote(kx_block(src), kx_block(src), kxs.at[0], kxr.at[src], re, pb).wait_recv()

    each(3, wait_kx)
    k_row = kx[0:16, :] + kx[16:32, :] + kx[32:48, :] + kx[48:64, :]
    turned = unfold(k_row, wide, 0)
    real, imag = turned[0:32], turned[32:64]
    group = iota((32, 128), 1) >> 5
    pieces = []
    for a in range(2):
        pieces.append(jnp.where(group == 2 * a, real, jnp.where(group == 2 * a + 1, imag, 0.0)))
        pieces.append(jnp.where(group == 2 * a, -imag, jnp.where(group == 2 * a + 1, real, 0.0)))
    rotation = split(jnp.concatenate(pieces, axis=0))

    def wait_a2(d):
        src = (y + d + 1) % 8
        remote(block(ra2, src), block(ra2, src), a2s_sem.at[0], a2r_sem.at[src], re, pb).wait_recv()

    each(7, wait_a2)
    ra2[pl.ds(pl.multiple_of(y * 48, 8), 48), :] = ra1[pl.ds(pl.multiple_of(y * 48, 8), 48), :]
    total = ra2[0:48, :]
    for source in range(1, 8):
        total = total + ra2[source * 48 : source * 48 + 48, :]
    def half_of(which):
        return ga.at[pl.ds(pl.multiple_of(which * 48, 8), 48), :]

    half_of(core)[...] = total
    a4 = remote(
        half_of(core), half_of(core), a4s_sem.at[0], a4r_sem.at[0], y * 2 + (1 - core), pb
    )
    a4.start()
    a4.wait_recv()
    padded = jnp.concatenate(
        [dot3(split(ga[...]), rotation, NN), jnp.zeros((32, 128), f32)], axis=0
    )
    turned_rows[...] = padded.T
    for n in range(2):
        for ac in range(4):
            a3s[pl.ds(n * 4 + ac, 8, stride=8), :] = turned_rows[
                pl.ds(ac * 32 + 2 * core + n, 8, stride=4), :
            ]

    def tile(ref, index):
        return ref.at[pl.ds(pl.multiple_of(index * 8, 8), 8), :]

    def a3(d):
        to = (y + d + 1) % 8
        return remote(
            tile(a3s, to), tile(a3r, y), a3s_sem.at[d], a3r_sem.at[y], to * 2 + core, pb
        )

    for d in FAR:
        a3(d).start()
    own_tile = pl.ds(pl.multiple_of(y * 8, 8), 8)
    a3r[own_tile, :] = a3s[own_tile, :]

    def wait_u1x(d):
        src = (x + d + 1) % 4
        remote(x_rows(src), x_rows(src), u1xs.at[0], u1xr.at[src], re, src * 8 + z).wait_recv()

    each(3, wait_u1x)

    def choose(i):
        k, q = i // 4, pb * 4 + i % 4
        index = (
            ((kco[0, k] + qco[0, q]) & 7) * 8 + ((kco[1, k] + qco[1, q]) & 7)
        ) * 8 + ((kco[2, k] + qco[2, q]) & 7)
        sel[pl.ds(i, 1), :] = table[pl.ds(index, 1), :]

    each(32, choose)

    def q_block(src):
        return usq.at[pl.ds(pl.multiple_of(src * 32, 8), 32), :]

    def uq(d):
        to = ((y + d + 1) % 8) * 2 + core
        return remote(sel.at[0:32, :], q_block(re), uqs.at[d], uqr.at[y], to, pb)

    usq[pl.ds(pl.multiple_of(re * 32, 8), 32), :] = sel[0:32, :]

    def uf(i):
        src = i * 2 + core
        return remote(q_block(src), q_block(src), ufs.at[i], ufr.at[i], y * 2 + (1 - core), pb)

    def wait_a3(d):
        src = (y + d + 1) % 8
        remote(tile(a3r, src), tile(a3r, src), a3s_sem.at[0], a3r_sem.at[src], re, pb).wait_recv()

    each(7, wait_a3)

    lane8 = iota((8, 128), 1)
    home = pl.multiple_of(pb * 48, 8)
    for n in range(2):
        v = [
            a3r[pl.ds(n * 4 + ac, 8, stride=8), :]
            for ac in range(4)
        ]
        r1, r2, r3 = pltpu.roll(v[1], 96, 1), pltpu.roll(v[2], 64, 1), pltpu.roll(v[3], 32, 1)
        thirds = [
            jnp.where(lane8 < 96, v[0], r1),
            jnp.where(lane8 < 64, r1, r2),
            jnp.where(lane8 < 32, r2, r3),
        ]
        for t in range(3):
            for kh in range(2):
                xs[pl.ds(home + kh * 24 + t * 8 + n * 4, 4), :] = thirds[t][kh * 4 : kh * 4 + 4]

    def chunk(src, kh):
        return xs.at[pl.ds(pl.multiple_of(src * 48 + kh * 24, 8), 24), :]

    def bx(kh, zs, d):
        src = x * 8 + zs
        return remote(
            chunk(src, kh), chunk(src, kh), bxs.at[kh * 24 + zs * 3 + d], bxr.at[kh * 32 + src],
            re, ((x + d + 1) % 4) * 8 + z,
        )

    def bz(kh, d):
        return remote(
            chunk(pb, kh), chunk(pb, kh), bzs.at[kh * 7 + d], bzr.at[kh * 8 + z],
            re, x * 8 + (z + d + 1) % 8,
        )

    for kh in range(2):
        for d in NEAR:
            bz(kh, d).start()
        for d in NEAR_X:
            bx(kh, z, d).start()
    for d in NEAR:
        uq(d).start()

    for kh in range(2):
        def pass_on(d):
            zs = (z + d + 1) % 8
            here = chunk(x * 8 + zs, kh)
            remote(here, here, bzs.at[0], bzr.at[kh * 8 + zs], re, pb).wait_recv()
            for e in NEAR_X:
                bx(kh, zs, e).start()

        for d in NEAR:
            pass_on(d)

    uf_own = uf(y)
    uf_own.start()

    def wait_uq(d):
        src = (y + d + 1) % 8
        here = q_block(src * 2 + core)
        remote(here, here, uqs.at[0], uqr.at[src], re, pb).wait_recv()
        uf(src).start()

    for d in NEAR:
        wait_uq(d)

    def wait_uf(i):
        here = q_block(i * 2 + (1 - core))
        remote(here, here, ufs.at[0], ufr.at[i], re, pb).wait_recv()

    each(8, wait_uf)

    def pair_matrices(kk):
        for q in range(4):
            for kl in range(2):
                value = unfold(
                    usq[pl.ds((2 * kk + kl) * 4 + q, 16, stride=32), :], wide, q * 2 + kl
                )
                for part in range(2):
                    for n in range(2):
                        kept = jnp.where(
                            group == 2 * kl + n, value[part * 32 : part * 32 + 32], 0.0
                        )
                        high, low = split(kept)
                        base = pl.multiple_of(
                            (kk * 4 + q) * 256 + part * 128 + kl * 64 + n * 32, 32
                        )
                        bh[pl.ds(base, 32), :] = high
                        bl[pl.ds(base, 32), :] = low

    each(4, pair_matrices)

    group24 = iota((24, 128), 1) >> 5
    row96 = iota((96, 128), 0)
    first = (
        (row96 < 12)
        | ((row96 >= 24) & (row96 < 36))
        | ((row96 >= 48) & (row96 < 60))
        | ((row96 >= 72) & (row96 < 84))
    )
    for kh in range(2):
        def wait_bx(i):
            src = ((x + i // 8 + 1) % 4) * 8 + i % 8
            here = chunk(src, kh)
            remote(here, here, bxs.at[0], bxr.at[kh * 32 + src], re, pb).wait_recv()

        each(24, wait_bx)

        for k4 in range(4):
            for n in range(2):
                for t in range(3):
                    high, low = split(xs[pl.ds(kh * 24 + t * 8 + n * 4 + k4, 32, stride=48), :])
                    to = k4 * 64 + n * 32
                    xh[to : to + 32, t * 128 : t * 128 + 128] = high
                    xl[to : to + 32, t * 128 : t * 128 + 128] = low
        result = dot3((fh[...], fl[...]), (xh[...], xl[...]), NT)
        ys[0:384, :] = result[:, 0:128]
        ys[384:768, :] = result[:, 128:256]

        def finish(kk):
            for q in range(4):
                value = ys[pl.ds(pl.multiple_of(kk * 384 + q * 96, 8), 96), :]
                other = jnp.where(first, pltpu.roll(value, 84, 0), -pltpu.roll(value, 12, 0))
                left = split(jnp.concatenate([value, other], axis=1))
                where = pl.ds(pl.multiple_of(((kh * 2 + kk) * 4 + q) * 256, 256), 256)
                res = dot3(left, (bh[where, :], bl[where, :]), NN)
                quarter = [res[j * 24 : j * 24 + 24] for j in range(4)]
                for kl in range(2):
                    for n in range(2):
                        to = 2 * kl + n
                        mixed = quarter[to]
                        for j in range(4):
                            if j != to:
                                shift = 32 * ((j - to) % 4)
                                mixed = jnp.where(
                                    group24 == j, pltpu.roll(quarter[j], shift, 1), mixed
                                )
                        k = kh * 4 + kk * 2 + kl
                        out[pl.ds((k * 4 + q) * 48 + n, 24, stride=2), :] = mixed

        each(2, finish)

    each(7, lambda d: u1z(d).wait_send())
    each(3, lambda d: u1x(d).wait_send())
    a1.wait_send()
    each(7, lambda d: a2(d).wait_send())
    each(7, lambda d: kz_copy(d).wait_send())
    each(3, lambda d: kx_copy(d).wait_send())
    each(7, lambda d: uq(d).wait_send())
    each(8, lambda d: uf(d).wait_send())
    a4.wait_send()
    each(7, lambda d: a3(d).wait_send())
    for kh in range(2):
        each(7, lambda d: bz(kh, d).wait_send())
        each(24, lambda i: bx(kh, i // 3, i % 3).wait_send())


def body(
    wannier_coupling,
    electron_cells,
    phonon_cells,
    kpoint_coords,
    qpoint_coords,
    band_rotations,
    mode_vectors,
):
    hbm = pl.BlockSpec(memory_space=pltpu.HBM)
    vmem = pl.BlockSpec(memory_space=pltpu.VMEM)
    V, S, D = pltpu.VMEM, pltpu.SMEM, pltpu.SemaphoreType.DMA
    result = pl.pallas_call(
        kernel,
        out_shape=pltpu.VMEM((1536, 128), f32),
        in_specs=[hbm] * 7,
        out_specs=vmem,
        scratch_shapes=[
            V((3, 32), i32),
            S((3, 4), i32),
            S((3, 8), i32),
            S((3, 128), i32),
            V((4, 4608), f32),
            V((192, 128), f32),
            V((256, 128), f32),
            V((3072, 128), f32),
            V((768, 128), f32),
            V((384, 128), f32),
            V((384, 128), f32),
            V((520, 128), f32),
            V((40, 128), f32),
            V((128, 128), f32),
            V((64, 128), f32),
            V((512, 128), f32),
            V((512, 128), f32),
            V((96, 128), f32),
            V((128, 128), f32),
            V((64, 128), f32),
            V((64, 128), f32),
            V((1544, 128), f32),
            V((392, 128), f32),
            V((384, 384), bf16),
            V((384, 384), bf16),
            V((4096, 128), bf16),
            V((4096, 128), bf16),
            V((256, 384), bf16),
            V((256, 384), bf16),
            V((768, 128), f32),
            D((1,)), D((16,)), D((5,)),
            D((7,)), D((8,)), D((3,)), D((4,)), D((1,)), D((1,)),
            D((7,)), D((8,)),
            D((7,)), D((8,)), D((3,)), D((4,)), D((7,)), D((8,)), D((8,)), D((8,)),
            D((1,)), D((1,)), D((7,)), D((8,)), D((14,)), D((16,)), D((48,)), D((64,)),
        ],
        compiler_params=pltpu.CompilerParams(
            collective_id=0, has_side_effects=True, vmem_limit_bytes=58 * 1024 * 1024
        ),
        name="interpolate",
    )(
        wannier_coupling.reshape(3072, 128),
        electron_cells,
        phonon_cells,
        kpoint_coords,
        qpoint_coords,
        band_rotations,
        mode_vectors,
    )
    return result.reshape(8, 4, 24, 2, 128).transpose(0, 1, 3, 2, 4).reshape(8, 4, 2, 3072)


def solution(mesh):
    return jax.shard_map(
        body,
        mesh=mesh,
        in_specs=(
            P("re", None, "pb", None),
            P(None, "re"),
            P(),
            P(),
            P(),
            P("pb", None),
            P("pb", None),
        ),
        out_specs=P(None, "pb", "re", None),
        check_vma=False,
    )
```

```python
import math

import jax
import jax.numpy as jnp
from jax import lax
from jax.experimental import pallas as pl
from jax.experimental.pallas import tpu as pltpu
from jax.sharding import PartitionSpec as P

f32, bf16, i32 = jnp.float32, jnp.bfloat16, jnp.int32
MESH = pl.DeviceIdType.MESH
NEAR = (0, 6, 1, 5, 2, 4, 3)
FAR = NEAR[::-1]
NEAR_X = (1, 0, 2)
NN = ((1,), (0,))
NT = ((1,), (1,))


def split(value):
    high = value.astype(bf16)
    return high, (value - high.astype(f32)).astype(bf16)


def dot(left, right, dims):
    return lax.dot_general(left, right, (dims, ((), ())), preferred_element_type=f32)


def dot3(left, right, dims):
    return (
        dot(left[0], right[0], dims) + dot(left[1], right[0], dims) + dot(left[0], right[1], dims)
    )


def iota(shape, axis):
    return lax.broadcasted_iota(i32, shape, axis)


def wave(turns, period):
    cosine = jnp.zeros(turns.shape, f32)
    sine = jnp.zeros(turns.shape, f32)
    for step in range(period):
        hit = turns == step
        angle = 2 * math.pi * step / period
        cosine = jnp.where(hit, jnp.float32(math.cos(angle)), cosine)
        sine = jnp.where(hit, jnp.float32(math.sin(angle)), sine)
    return cosine, sine


def unfold(slices, wide, region):
    group = iota((16, 128), 1) >> 5
    for j in range(4):
        wide[pl.ds(region * 64 + j, 16, stride=4), :] = jnp.where(group == j, slices, 0.0)
    kept = wide[region * 64 : region * 64 + 64, :]
    kept = kept + pltpu.roll(kept, 64, 1)
    return kept + pltpu.roll(kept, 32, 1)


def kernel(
    g_hbm, cells_hbm, pcell_hbm, kco_hbm, qco_hbm, rot_hbm, modes_hbm, out,
    cells, pcell, kco, qco, flat, modes, rot, g, acc, ra1, ra2, table, sel, kz, kx, usq, wide,
    ga, turned_rows, a3s, a3r, xs, fq, fh, fl, bh, bl, xh, xl, ys,
    gsem, rotsem, insem, u1zs, u1zr, u1xs, u1xr, a1s_sem, a1r_sem, a2s_sem, a2r_sem,
    kzs, kzr, kxs, kxr, uqs, uqr, ufs, ufr, a4s_sem, a4r_sem, a3s_sem, a3r_sem, bzs, bzr, bxs, bxr,
):
    re = lax.axis_index("re")
    pb = lax.axis_index("pb")
    y, core = re // 2, re % 2
    x, z = pb // 8, pb % 8

    def remote(src, dst, ssem, rsem, to_re, to_pb):
        return pltpu.make_async_remote_copy(
            src_ref=src, dst_ref=dst, send_sem=ssem, recv_sem=rsem,
            device_id=(to_re, to_pb), device_id_type=MESH,
        )

    def each(count, body):
        def step(i, carry):
            body(i)
            return carry

        lax.fori_loop(0, count, step, 0)

    barrier = pltpu.get_barrier_semaphore()

    def greet_y(d):
        pl.semaphore_signal(
            barrier, 1, device_id=(((y + d + 1) % 8) * 2 + core, pb), device_id_type=MESH
        )

    def greet_z(d):
        pl.semaphore_signal(
            barrier, 1, device_id=(re, x * 8 + (z + d + 1) % 8), device_id_type=MESH
        )

    def greet_x(d):
        pl.semaphore_signal(
            barrier, 1, device_id=(re, ((x + d + 1) % 4) * 8 + z), device_id_type=MESH
        )

    for d in NEAR[::-1]:
        greet_y(d)
        greet_z(d)
    each(3, greet_x)
    pl.semaphore_signal(barrier, 1, device_id=(y * 2 + (1 - core), pb), device_id_type=MESH)
    small = [
        pltpu.make_async_copy(src, dst, insem.at[i])
        for i, (src, dst) in enumerate(
            [(kco_hbm, kco), (cells_hbm, cells), (pcell_hbm, pcell), (qco_hbm, qco)]
        )
    ]
    modes_copy = pltpu.make_async_copy(modes_hbm, flat, insem.at[4])

    def rot_copy(i):
        return pltpu.make_async_copy(
            rot_hbm.at[:, pl.ds(pl.multiple_of(i * 128, 128), 128)],
            rot.at[pl.ds(pl.multiple_of(i * 16, 16), 16), :],
            rotsem.at[i],
        )

    g_copy = pltpu.make_async_copy(g_hbm, g, gsem.at[0])
    g_copy.start()
    for copy in small:
        copy.start()
    each(16, lambda i: rot_copy(i).start())
    own_rows = table.at[pl.ds(pl.multiple_of(pb * 16, 16), 16), :]
    modes_copy.start()

    for copy in small:
        copy.wait()

    row = iota((8, 64), 0)
    turns = jnp.zeros((8, 64), i32)
    twice = jnp.concatenate([cells[...], cells[...]], axis=1)
    for d in range(3):
        coef = jnp.zeros((8, 64), i32)
        for k in range(8):
            coef = jnp.where(row == k, 2 * kco[d, k] + 1, coef)
        turns = turns + coef * jnp.broadcast_to(twice[d : d + 1, :], (8, 64))
    cosine, sine = wave(turns & 15, 16)
    waves = jnp.concatenate(split(jnp.concatenate([cosine, sine], axis=0)), axis=0)

    k_index = ((kco[0, y] & 7) * 8 + (kco[1, y] & 7)) * 8 + (kco[2, y] & 7)
    each(16, lambda i: rot_copy(i).wait())
    held = jnp.full((16, 128), k_index >> 4, i32) == jnp.full((16, 128), pb, i32)

    def kz_block(src):
        return kz.at[pl.ds(pl.multiple_of(src * 16, 16), 16), :]

    def kx_block(src):
        return kx.at[pl.ds(pl.multiple_of(src * 16, 16), 16), :]

    kz[pl.ds(pl.multiple_of(z * 16, 16), 16), :] = jnp.where(
        held, rot[pl.ds(k_index & 15, 16, stride=16), :], 0.0
    )
    own_rows[...] = rot[pl.ds(pl.multiple_of(re * 16, 16), 16), :]

    odd = ((iota((8, 128), 1) >> 5) & 1) == 1

    def phase_part(half, pp):
        for i in range(12):
            highs, lows = [], []
            for lo in range(2):
                start = half * 48 + pp * 24 + 2 * i + lo
                high, low = split(g[pl.ds(start, 32, stride=96), :])
                highs.append(high)
                lows.append(low)
            stacked = jnp.concatenate(
                [jnp.concatenate(highs, axis=1), jnp.concatenate(lows, axis=1)], axis=0
            )
            both = dot(waves, stacked, NN)
            both = both[0:16] + both[16:32]
            for lo in range(2):
                real = both[0:8, lo * 128 : lo * 128 + 128]
                turned = both[8:16, lo * 128 : lo * 128 + 128]
                swapped = jnp.where(odd, pltpu.roll(turned, 32, 1), -pltpu.roll(turned, 96, 1))
                acc[pl.ds(half * 384 + pp * 24 + lo * 12 + i, 8, stride=48), :] = real + swapped

    g_copy.wait()
    for pp in range(2):
        phase_part(1 - core, pp)
    for pp in range(2):
        phase_part(core, pp)
    pl.semaphore_wait(barrier, 18)
    def kz_copy(d):
        return remote(
            kz_block(z), kz_block(z), kzs.at[d], kzr.at[z], re, x * 8 + (z + d + 1) % 8
        )

    for d in FAR:
        kz_copy(d).start()
    a1 = remote(
        acc.at[pl.ds(pl.multiple_of((1 - core) * 384, 8), 384), :], ra1,
        a1s_sem.at[0], a1r_sem.at[0], y * 2 + (1 - core), pb,
    )
    a1.start()

    def u1z(d):
        return remote(
            own_rows, own_rows, u1zs.at[d], u1zr.at[z], re, x * 8 + (z + d + 1) % 8
        )


    a1.wait_recv()
    mine = pl.multiple_of(core * 384, 8)
    ra1[...] = ra1[...] + acc[pl.ds(mine, 384), :]

    def block(ref, index):
        return ref.at[pl.ds(pl.multiple_of(index * 48, 8), 48), :]

    def a2(d):
        to = (y + d + 1) % 8
        return remote(block(ra1, to), block(ra2, y), a2s_sem.at[d], a2r_sem.at[y], to * 2 + core, pb)

    for d in FAR:
        a2(d).start()
    for d in NEAR:
        u1z(d).start()

    def wait_kz(d):
        src = (z + d + 1) % 8
        remote(kz_block(src), kz_block(src), kzs.at[0], kzr.at[src], re, pb).wait_recv()

    each(7, wait_kz)
    found = kz[0:16, :]
    for s in range(1, 8):
        found = found + kz[s * 16 : s * 16 + 16, :]
    kx[pl.ds(pl.multiple_of(x * 16, 16), 16), :] = found

    def kx_copy(d):
        return remote(
            kx_block(x), kx_block(x), kxs.at[d], kxr.at[x], re, ((x + d + 1) % 4) * 8 + z
        )

    each(3, lambda d: kx_copy(d).start())

    def z_rows(src):
        return table.at[pl.ds(pl.multiple_of((x * 8 + src) * 16, 16), 16), :]

    def wait_u1z(d):
        src = (z + d + 1) % 8
        remote(z_rows(src), z_rows(src), u1zs.at[0], u1zr.at[src], re, x * 8 + src).wait_recv()

    each(7, wait_u1z)

    def x_rows(src):
        return table.at[pl.ds(pl.multiple_of(src * 128, 128), 128), :]

    def u1x(d):
        return remote(x_rows(x), x_rows(x), u1xs.at[d], u1xr.at[x], re, ((x + d + 1) % 4) * 8 + z)

    each(3, lambda d: u1x(d).start())

    modes_copy.wait()
    for tile_index in range(36):
        modes[tile_index * 4 : tile_index * 4 + 4, :] = flat[
            :, tile_index * 128 : tile_index * 128 + 128
        ]
    lane12 = iota((12, 128), 1)
    permute_row = iota((96, 128), 0)
    block24 = (
        (permute_row >= 24).astype(i32)
        + (permute_row >= 48).astype(i32)
        + (permute_row >= 72).astype(i32)
    )
    rest = permute_row - 24 * block24
    part = (rest >= 12).astype(i32)
    target = part * 48 + 4 * (rest - 12 * part) + block24
    permute = (iota((96, 128), 1) == target).astype(f32).astype(bf16)

    def mode_q(q):
        v = [modes[pl.ds(tt * 4 + q, 12, stride=12), :] for tt in range(3)]
        r0, r1, r2 = pltpu.roll(v[0], 32, 1), pltpu.roll(v[1], 32, 1), pltpu.roll(v[1], 64, 1)
        r3, r4 = pltpu.roll(v[2], 64, 1), pltpu.roll(v[2], 96, 1)
        raw = [
            v[0],
            jnp.where(lane12 < 32, r0, r1),
            jnp.where(lane12 < 64, r2, r3),
            r4,
        ]
        plain, crossed = [], []
        for value in raw:
            value = jnp.where(lane12 < 96, value, 0.0)
            other = jnp.where(lane12 < 48, -pltpu.roll(value, 80, 1), pltpu.roll(value, 48, 1))
            plain.append(value)
            crossed.append(jnp.where(lane12 < 96, other, 0.0))
        point = pb * 4 + q
        for p in range(4):
            turn = (
                qco[0, point] * pcell[0, p]
                + qco[1, point] * pcell[1, p]
                + qco[2, point] * pcell[2, p]
            ) & 7
            cos_p, sin_p = wave(jnp.full((1, 128), turn, i32), 8)
            for a2 in range(2):
                for lo in range(2):
                    i = 2 * lo + a2
                    base = a2 * 192 + p * 24 + lo * 12
                    fq[base : base + 12, :] = cos_p * plain[i] + sin_p * crossed[i]
                    fq[base + 96 : base + 108, :] = cos_p * crossed[i] - sin_p * plain[i]
        high, low = split(fq[0:384, :])
        where = pl.ds(pl.multiple_of(q * 96, 96), 96)
        fh[where, :] = dot(permute, high, NT).astype(bf16)
        fl[where, :] = dot(permute, low, NT).astype(bf16)

    each(4, mode_q)

    def wait_kx(d):
        src = (x + d + 1) % 4
        remote(kx_block(src), kx_block(src), kxs.at[0], kxr.at[src], re, pb).wait_recv()

    each(3, wait_kx)
    k_row = kx[0:16, :] + kx[16:32, :] + kx[32:48, :] + kx[48:64, :]
    turned = unfold(k_row, wide, 0)
    real, imag = turned[0:32], turned[32:64]
    group = iota((32, 128), 1) >> 5
    pieces = []
    for a in range(2):
        pieces.append(jnp.where(group == 2 * a, real, jnp.where(group == 2 * a + 1, imag, 0.0)))
        pieces.append(jnp.where(group == 2 * a, -imag, jnp.where(group == 2 * a + 1, real, 0.0)))
    rotation = split(jnp.concatenate(pieces, axis=0))

    def wait_a2(d):
        src = (y + d + 1) % 8
        remote(block(ra2, src), block(ra2, src), a2s_sem.at[0], a2r_sem.at[src], re, pb).wait_recv()

    each(7, wait_a2)
    ra2[pl.ds(pl.multiple_of(y * 48, 8), 48), :] = ra1[pl.ds(pl.multiple_of(y * 48, 8), 48), :]
    total = ra2[0:48, :]
    for source in range(1, 8):
        total = total + ra2[source * 48 : source * 48 + 48, :]
    def half_of(which):
        return ga.at[pl.ds(pl.multiple_of(which * 48, 8), 48), :]

    half_of(core)[...] = total
    a4 = remote(
        half_of(core), half_of(core), a4s_sem.at[0], a4r_sem.at[0], y * 2 + (1 - core), pb
    )
    a4.start()
    a4.wait_recv()
    padded = jnp.concatenate(
        [dot3(split(ga[...]), rotation, NN), jnp.zeros((32, 128), f32)], axis=0
    )
    turned_rows[...] = padded.T
    for n in range(2):
        for ac in range(4):
            a3s[pl.ds(n * 4 + ac, 8, stride=8), :] = turned_rows[
                pl.ds(ac * 32 + 2 * core + n, 8, stride=4), :
            ]

    def tile(ref, index):
        return ref.at[pl.ds(pl.multiple_of(index * 8, 8), 8), :]

    def a3(d):
        to = (y + d + 1) % 8
        return remote(
            tile(a3s, to), tile(a3r, y), a3s_sem.at[d], a3r_sem.at[y], to * 2 + core, pb
        )

    for d in FAR:
        a3(d).start()
    own_tile = pl.ds(pl.multiple_of(y * 8, 8), 8)
    a3r[own_tile, :] = a3s[own_tile, :]

    def wait_u1x(d):
        src = (x + d + 1) % 4
        remote(x_rows(src), x_rows(src), u1xs.at[0], u1xr.at[src], re, src * 8 + z).wait_recv()

    each(3, wait_u1x)

    def choose(i):
        k, q = i // 4, pb * 4 + i % 4
        index = (
            ((kco[0, k] + qco[0, q]) & 7) * 8 + ((kco[1, k] + qco[1, q]) & 7)
        ) * 8 + ((kco[2, k] + qco[2, q]) & 7)
        sel[pl.ds(i, 1), :] = table[pl.ds(index, 1), :]

    each(32, choose)

    def q_block(src):
        return usq.at[pl.ds(pl.multiple_of(src * 32, 8), 32), :]

    def uq(d):
        to = ((y + d + 1) % 8) * 2 + core
        return remote(sel.at[0:32, :], q_block(re), uqs.at[d], uqr.at[y], to, pb)

    usq[pl.ds(pl.multiple_of(re * 32, 8), 32), :] = sel[0:32, :]

    def uf(i):
        src = i * 2 + core
        return remote(q_block(src), q_block(src), ufs.at[i], ufr.at[i], y * 2 + (1 - core), pb)

    def wait_a3(d):
        src = (y + d + 1) % 8
        remote(tile(a3r, src), tile(a3r, src), a3s_sem.at[0], a3r_sem.at[src], re, pb).wait_recv()

    each(7, wait_a3)

    lane8 = iota((8, 128), 1)
    home = pl.multiple_of(pb * 48, 8)
    for n in range(2):
        v = [
            a3r[pl.ds(n * 4 + ac, 8, stride=8), :]
            for ac in range(4)
        ]
        r1, r2, r3 = pltpu.roll(v[1], 96, 1), pltpu.roll(v[2], 64, 1), pltpu.roll(v[3], 32, 1)
        thirds = [
            jnp.where(lane8 < 96, v[0], r1),
            jnp.where(lane8 < 64, r1, r2),
            jnp.where(lane8 < 32, r2, r3),
        ]
        for t in range(3):
            for kh in range(2):
                xs[pl.ds(home + kh * 24 + t * 8 + n * 4, 4), :] = thirds[t][kh * 4 : kh * 4 + 4]

    def chunk(src, kh):
        return xs.at[pl.ds(pl.multiple_of(src * 48 + kh * 24, 8), 24), :]

    def bx(kh, zs, d):
        src = x * 8 + zs
        return remote(
            chunk(src, kh), chunk(src, kh), bxs.at[kh * 24 + zs * 3 + d], bxr.at[kh * 32 + src],
            re, ((x + d + 1) % 4) * 8 + z,
        )

    def bz(kh, d):
        return remote(
            chunk(pb, kh), chunk(pb, kh), bzs.at[kh * 7 + d], bzr.at[kh * 8 + z],
            re, x * 8 + (z + d + 1) % 8,
        )

    for kh in range(2):
        for d in NEAR:
            bz(kh, d).start()
        for d in NEAR_X:
            bx(kh, z, d).start()
    for d in NEAR:
        uq(d).start()

    for kh in range(2):
        def pass_on(d):
            zs = (z + d + 1) % 8
            here = chunk(x * 8 + zs, kh)
            remote(here, here, bzs.at[0], bzr.at[kh * 8 + zs], re, pb).wait_recv()
            for e in NEAR_X:
                bx(kh, zs, e).start()

        for d in NEAR:
            pass_on(d)

    uf_own = uf(y)
    uf_own.start()

    def wait_uq(d):
        src = (y + d + 1) % 8
        here = q_block(src * 2 + core)
        remote(here, here, uqs.at[0], uqr.at[src], re, pb).wait_recv()
        uf(src).start()

    for d in NEAR:
        wait_uq(d)

    def wait_uf(i):
        here = q_block(i * 2 + (1 - core))
        remote(here, here, ufs.at[0], ufr.at[i], re, pb).wait_recv()

    each(8, wait_uf)

    def pair_matrices(kk):
        for q in range(4):
            for kl in range(2):
                value = unfold(
                    usq[pl.ds((2 * kk + kl) * 4 + q, 16, stride=32), :], wide, q * 2 + kl
                )
                for part in range(2):
                    for n in range(2):
                        kept = jnp.where(
                            group == 2 * kl + n, value[part * 32 : part * 32 + 32], 0.0
                        )
                        high, low = split(kept)
                        base = pl.multiple_of(
                            (kk * 4 + q) * 256 + part * 128 + kl * 64 + n * 32, 32
                        )
                        bh[pl.ds(base, 32), :] = high
                        bl[pl.ds(base, 32), :] = low

    each(4, pair_matrices)

    group24 = iota((24, 128), 1) >> 5
    row96 = iota((96, 128), 0)
    first = (
        (row96 < 12)
        | ((row96 >= 24) & (row96 < 36))
        | ((row96 >= 48) & (row96 < 60))
        | ((row96 >= 72) & (row96 < 84))
    )
    for kh in range(2):
        def wait_bx(i):
            src = ((x + i // 8 + 1) % 4) * 8 + i % 8
            here = chunk(src, kh)
            remote(here, here, bxs.at[0], bxr.at[kh * 32 + src], re, pb).wait_recv()

        each(24, wait_bx)

        for k4 in range(4):
            for n in range(2):
                for t in range(3):
                    high, low = split(xs[pl.ds(kh * 24 + t * 8 + n * 4 + k4, 32, stride=48), :])
                    to = k4 * 64 + n * 32
                    xh[to : to + 32, t * 128 : t * 128 + 128] = high
                    xl[to : to + 32, t * 128 : t * 128 + 128] = low
        result = dot3((fh[...], fl[...]), (xh[...], xl[...]), NT)
        ys[0:384, :] = result[:, 0:128]
        ys[384:768, :] = result[:, 128:256]

        def finish(kk):
            for q in range(4):
                value = ys[pl.ds(pl.multiple_of(kk * 384 + q * 96, 8), 96), :]
                other = jnp.where(first, pltpu.roll(value, 84, 0), -pltpu.roll(value, 12, 0))
                left = split(jnp.concatenate([value, other], axis=1))
                where = pl.ds(pl.multiple_of(((kh * 2 + kk) * 4 + q) * 256, 256), 256)
                res = dot3(left, (bh[where, :], bl[where, :]), NN)
                quarter = [res[j * 24 : j * 24 + 24] for j in range(4)]
                for kl in range(2):
                    for n in range(2):
                        to = 2 * kl + n
                        mixed = quarter[to]
                        for j in range(4):
                            if j != to:
                                shift = 32 * ((j - to) % 4)
                                mixed = jnp.where(
                                    group24 == j, pltpu.roll(quarter[j], shift, 1), mixed
                                )
                        k = kh * 4 + kk * 2 + kl
                        out[pl.ds((k * 4 + q) * 48 + n, 24, stride=2), :] = mixed

        each(2, finish)

    each(7, lambda d: u1z(d).wait_send())
    each(3, lambda d: u1x(d).wait_send())
    a1.wait_send()
    each(7, lambda d: a2(d).wait_send())
    each(7, lambda d: kz_copy(d).wait_send())
    each(3, lambda d: kx_copy(d).wait_send())
    each(7, lambda d: uq(d).wait_send())
    each(8, lambda d: uf(d).wait_send())
    a4.wait_send()
    each(7, lambda d: a3(d).wait_send())
    for kh in range(2):
        each(7, lambda d: bz(kh, d).wait_send())
        each(24, lambda i: bx(kh, i // 3, i % 3).wait_send())


def body(
    wannier_coupling,
    electron_cells,
    phonon_cells,
    kpoint_coords,
    qpoint_coords,
    band_rotations,
    mode_vectors,
):
    hbm = pl.BlockSpec(memory_space=pltpu.HBM)
    vmem = pl.BlockSpec(memory_space=pltpu.VMEM)
    V, S, D = pltpu.VMEM, pltpu.SMEM, pltpu.SemaphoreType.DMA
    result = pl.pallas_call(
        kernel,
        out_shape=pltpu.VMEM((1536, 128), f32),
        in_specs=[hbm] * 7,
        out_specs=vmem,
        scratch_shapes=[
            V((3, 32), i32),
            S((3, 4), i32),
            S((3, 8), i32),
            S((3, 128), i32),
            V((4, 4608), f32),
            V((192, 128), f32),
            V((256, 128), f32),
            V((3072, 128), f32),
            V((768, 128), f32),
            V((384, 128), f32),
            V((384, 128), f32),
            V((520, 128), f32),
            V((40, 128), f32),
            V((128, 128), f32),
            V((64, 128), f32),
            V((512, 128), f32),
            V((512, 128), f32),
            V((96, 128), f32),
            V((128, 128), f32),
            V((64, 128), f32),
            V((64, 128), f32),
            V((1544, 128), f32),
            V((392, 128), f32),
            V((384, 384), bf16),
            V((384, 384), bf16),
            V((4096, 128), bf16),
            V((4096, 128), bf16),
            V((256, 384), bf16),
            V((256, 384), bf16),
            V((768, 128), f32),
            D((1,)), D((16,)), D((5,)),
            D((7,)), D((8,)), D((3,)), D((4,)), D((1,)), D((1,)),
            D((7,)), D((8,)),
            D((7,)), D((8,)), D((3,)), D((4,)), D((7,)), D((8,)), D((8,)), D((8,)),
            D((1,)), D((1,)), D((7,)), D((8,)), D((14,)), D((16,)), D((48,)), D((64,)),
        ],
        compiler_params=pltpu.CompilerParams(
            collective_id=0, has_side_effects=True, vmem_limit_bytes=58 * 1024 * 1024
        ),
        name="interpolate",
    )(
        wannier_coupling.reshape(3072, 128),
        electron_cells,
        phonon_cells,
        kpoint_coords,
        qpoint_coords,
        band_rotations,
        mode_vectors,
    )
    return result.reshape(8, 4, 24, 2, 128).transpose(0, 1, 3, 2, 4).reshape(8, 4, 2, 3072)


def solution(mesh):
    return jax.shard_map(
        body,
        mesh=mesh,
        in_specs=(
            P("re", None, "pb", None),
            P(None, "re"),
            P(),
            P(),
            P(),
            P("pb", None),
            P("pb", None),
        ),
        out_specs=P(None, "pb", "re", None),
        check_vma=False,
    )
```
